256 devices in a mesh: patch: 32 (over y, x, core), sub: 8 (over z).
Axes of the slice: x: 4, y: 4, z: 8, core: 2. Of those that a mesh axis runs over, the one named last changes fastest.
Arguments:
- nodes: bfloat16 [32768, 512], P(('patch', 'sub')), may hold values from -6 to 6
- fine_edges: bfloat16 [196608, 512], P(('patch', 'sub')), may hold values from -6 to 6
- long_edges: bfloat16 [65536, 512], P(('patch', 'sub')), may hold values from -6 to 6
- fine_send: int32 [196608], P(('patch', 'sub')), may hold values from 0 to 447
- fine_recv: int32 [196608], P(('patch', 'sub')), may hold values from 0 to 127
- long_send: int32 [65536], P(('patch', 'sub')), may hold values from 0 to 2047, as said below
- long_recv: int32 [65536], P(('patch', 'sub')), may hold values from 0 to 7
- long_mask: int32 [65536], P(('patch', 'sub')), may hold values from 0 to 1, as said below
- sub_list: int32 [2048, 32], P(('patch', 'sub')), may hold values from 0 to 127
- patch_list: int32 [512, 32], P(('patch', 'sub')), may hold values from 0 to 127
- edge_w1: bfloat16 [1536, 512], replicated, may hold values from -0.15625 to 0.15625
- edge_w2: bfloat16 [512, 512], replicated, may hold values from -0.25 to 0.25
- node_w1: bfloat16 [1024, 512], replicated, may hold values from -0.1875 to 0.1875
- node_w2: bfloat16 [512, 512], replicated, may hold values from -0.25 to 0.25
- upstream_nodes: bfloat16 [32768, 512], P(('patch', 'sub')), may hold values from -6 to 6
- upstream_fine: bfloat16 [196608, 512], P(('patch', 'sub')), may hold values from -6 to 6
- upstream_long: bfloat16 [65536, 512], P(('patch', 'sub')), may hold values from -6 to 6
Outputs:
- new_nodes: bfloat16 [32768, 512], P(('patch', 'sub'))
- new_fine: bfloat16 [196608, 512], P(('patch', 'sub'))
- new_long: bfloat16 [65536, 512], P(('patch', 'sub'))
- grad_nodes: bfloat16 [32768, 512], P(('patch', 'sub'))
- grad_fine: bfloat16 [196608, 512], P(('patch', 'sub'))
- grad_long: bfloat16 [65536, 512], P(('patch', 'sub'))
- grad_edge_first: float32 [1536, 512], P('patch')
- grad_edge_second: float32 [512, 512], P('patch')
- grad_node_first: float32 [1024, 512], P('patch')
- grad_node_second: float32 [512, 512], P('patch')
The draws below stay inside these ranges and needn't reach their ends.
Inputs may be any that keep to these rules, and one draw needn't show every extreme that they name: `long_mask`: within the 256 slots of one block the live long edges come first; some block has all slots live. `long_send`: any coarse node may send to any block.
All inputs are finite; a program needn't handle non-finite values.
Results may differ from the reference program's by a relative error of at most 0.03.
Values may be sent and summed in bfloat16 or wider, within the bound.
A program may use at most 128 MiB of HBM per device.

```python
import jax
import jax.numpy as jnp
from jax import lax

D = 512
NODE_DEV = 128
COARSE_DEV = 8
HB = 32
LONG_CAP = 256
FINE_DEV = 768
NODES = 32768
FINE_E = 196608
LONG_E = 65536
EXT = 448
SUB_LISTS = 2048
PATCH_LISTS = 512
N_PATCH = 32
N_SUB = 8
DEVICES = 256


def draw_long_mask(key, part):
    key = jax.random.fold_in(key, 11)
    key_counts, key_full, key_pick = jax.random.split(key, 3)
    counts = jax.random.randint(key_counts, (DEVICES,), LONG_CAP // 4, 3 * LONG_CAP // 4 + 1)
    full = jax.random.randint(key_full, (DEVICES,), 0, 6) == 0
    chosen = jax.random.randint(key_pick, (), 0, DEVICES)
    counts = jnp.where(full, LONG_CAP, counts)
    counts = jnp.where(jnp.arange(DEVICES) == chosen, LONG_CAP, counts)
    slots = jnp.arange(LONG_CAP)[None, :] < counts[:, None]
    return slots.astype(jnp.int32).reshape(-1)


def draw_long_send(key, part):
    key = jax.random.fold_in(key, 5)
    key_local, key_any = jax.random.split(key, 2)
    positions = jnp.arange(DEVICES * LONG_CAP, dtype=jnp.int32)
    owner = positions // LONG_CAP
    slot = positions % LONG_CAP
    far_block = (owner + DEVICES // 2) % DEVICES
    local_row = jax.random.randint(key_local, (DEVICES * LONG_CAP,), 0, COARSE_DEV)
    anywhere = jax.random.randint(key_any, (DEVICES * LONG_CAP,), 0, COARSE_DEV * DEVICES)
    picked = jnp.where(slot % 4 == 0, anywhere, far_block * COARSE_DEV + local_row)
    return picked.astype(jnp.int32)


def plant(drawn, own_key, low, largest):
    longest = drawn.shape.index(max(drawn.shape))
    spots = []
    for shift in (0, 1):
        where = [jax.random.randint(jax.random.fold_in(own_key, axis), (), 0, length) for axis, length in enumerate(drawn.shape)]
        where[longest] = (where[longest] + shift) % drawn.shape[longest]
        spots.append(tuple(where))
    return drawn.at[spots[0]].set(low).at[spots[1]].set(largest)


def steps_of(own_key, dims, cuts, smallest, high):
    loudness, own = 1.0, jax.random.fold_in(own_key, 6)
    for dim, blocks in cuts:
        heights = jnp.exp(jax.random.uniform(jax.random.fold_in(own, dim), (blocks,), jnp.float32, smallest / len(cuts), high / len(cuts)))
        loudness = loudness * jnp.repeat(heights, dims[dim] // blocks).reshape([-1 if axis == dim else 1 for axis in range(len(dims))])
    return loudness


def centred(own_key, extent, width, reach, shards=(), kind=jnp.bfloat16):
    values = jax.random.normal(own_key, extent, jnp.float32) * width
    if len(shards) > 0:
        values = steps_of(own_key, extent, shards, -0.22, 0.18) * values
    return jnp.clip(values, min=-reach, max=reach).astype(kind)


def setup_inputs(seed: int = 0) -> dict:
    splits = jax.random.split(jax.random.key(seed), 18)
    return {
        "nodes": centred(splits[0], (NODES, D), 1.0, 6.0, ((0, 256),)),
        "fine_edges": centred(splits[1], (FINE_E, D), 1.0, 6.0, ((0, 256),)),
        "long_edges": centred(splits[2], (LONG_E, D), 1.0, 6.0, ((0, 256),)),
        "fine_send": plant(jax.random.randint(splits[3], (FINE_E,), 0, EXT), jax.random.fold_in(splits[3], 1), 0, EXT - 1).astype(jnp.int32),
        "fine_recv": plant(jax.random.randint(splits[4], (FINE_E,), 0, NODE_DEV), jax.random.fold_in(splits[4], 1), 0, NODE_DEV - 1).astype(jnp.int32),
        "long_send": draw_long_send(jax.random.fold_in(splits[17], 71), 0),
        "long_recv": plant(jax.random.randint(splits[6], (LONG_E,), 0, COARSE_DEV), jax.random.fold_in(splits[6], 1), 0, COARSE_DEV - 1).astype(jnp.int32),
        "long_mask": draw_long_mask(jax.random.fold_in(splits[17], 71), 0),
        "sub_list": plant(jax.random.randint(splits[8], (SUB_LISTS, HB), 0, NODE_DEV), jax.random.fold_in(splits[8], 1), 0, NODE_DEV - 1).astype(jnp.int32),
        "patch_list": plant(jax.random.randint(splits[9], (PATCH_LISTS, HB), 0, NODE_DEV), jax.random.fold_in(splits[9], 1), 0, NODE_DEV - 1).astype(jnp.int32),
        "edge_w1": centred(splits[10], (3 * D, D), (3 * D) ** -0.5, 0.15625),
        "edge_w2": centred(splits[11], (D, D), D ** -0.5, 0.25),
        "node_w1": centred(splits[12], (2 * D, D), (2 * D) ** -0.5, 0.1875),
        "node_w2": centred(splits[13], (D, D), D ** -0.5, 0.25),
        "upstream_nodes": centred(splits[14], (NODES, D), 1.0, 6.0, ((0, 256),)),
        "upstream_fine": centred(splits[15], (FINE_E, D), 1.0, 6.0, ((0, 256),)),
        "upstream_long": centred(splits[16], (LONG_E, D), 1.0, 6.0, ((0, 256),)),
    }


eps = 1e-05

def silu_slope(values):
    sigma = jax.nn.sigmoid(values)
    return sigma + values * sigma * (1.0 - sigma)

def norm_rows(values):
    row_mean = lax.optimization_barrier(jnp.mean(values, axis=-1, keepdims=True))
    centered = values - row_mean
    inverse = lax.rsqrt(lax.optimization_barrier(jnp.mean(centered * centered, axis=-1, keepdims=True)) + eps)
    return (centered * inverse, inverse)

def norm_back(normed, inverse, upstream):
    mean_grad = lax.optimization_barrier(jnp.mean(upstream, axis=-1, keepdims=True))
    mean_prod = lax.optimization_barrier(jnp.mean(upstream * normed, axis=-1, keepdims=True))
    return (upstream - mean_grad - normed * mean_prod) * inverse

def contract(left, right):
    return lax.dot_general(left, right, (((0,), (0,)), ((), ())), preferred_element_type=jnp.float32)

def layer_pass(nodes, edge_in, recv_all, live_all, edge_w1, edge_w2, node_w1, node_w2, upstream_nodes, upstream_edges):
    features = nodes.shape[1]
    node_count = nodes.shape[0]
    edge_first = jnp.dot(edge_in, edge_w1, preferred_element_type=jnp.float32)
    edge_active = jax.nn.silu(edge_first).astype(jnp.bfloat16)
    edge_second = jnp.dot(edge_active, edge_w2, preferred_element_type=jnp.float32)
    edge_normed, edge_inverse = norm_rows(edge_second)
    new_edges = (edge_in[:, :features].astype(jnp.float32) + live_all * edge_normed).astype(jnp.bfloat16)
    aggregate = jax.ops.segment_sum(live_all * new_edges.astype(jnp.float32), recv_all, num_segments=node_count)
    aggregate = aggregate.astype(jnp.bfloat16)
    node_in = jnp.concatenate([nodes, aggregate], axis=1)
    node_first = jnp.dot(node_in, node_w1, preferred_element_type=jnp.float32)
    node_active = jax.nn.silu(node_first).astype(jnp.bfloat16)
    node_second = jnp.dot(node_active, node_w2, preferred_element_type=jnp.float32)
    node_normed, node_inverse = norm_rows(node_second)
    new_nodes = (nodes.astype(jnp.float32) + node_normed).astype(jnp.bfloat16)
    upstream_node_rows = upstream_nodes.astype(jnp.float32)
    node_grad_second = norm_back(node_normed, node_inverse, upstream_node_rows).astype(jnp.bfloat16)
    grad_node_second = contract(node_active, node_grad_second)
    node_grad_first = jnp.dot(node_grad_second, node_w2.T, preferred_element_type=jnp.float32) * silu_slope(node_first)
    node_grad_first = node_grad_first.astype(jnp.bfloat16)
    grad_node_first = contract(node_in, node_grad_first)
    node_grad_in = jnp.dot(node_grad_first, node_w1.T, preferred_element_type=jnp.float32)
    grad_aggregate = node_grad_in[:, features:]
    edge_grad_new = upstream_edges.astype(jnp.float32) + live_all * jnp.take(grad_aggregate, recv_all, axis=0)
    edge_grad_second = (live_all * norm_back(edge_normed, edge_inverse, edge_grad_new)).astype(jnp.bfloat16)
    grad_edge_second = contract(edge_active, edge_grad_second)
    edge_grad_first = jnp.dot(edge_grad_second, edge_w2.T, preferred_element_type=jnp.float32) * silu_slope(edge_first)
    edge_grad_first = edge_grad_first.astype(jnp.bfloat16)
    grad_edge_first = contract(edge_in, edge_grad_first)
    edge_grad_in = jnp.dot(edge_grad_first, edge_w1.T, preferred_element_type=jnp.float32)
    grad_edges = (edge_grad_new + edge_grad_in[:, :features]).astype(jnp.bfloat16)
    grad_local = upstream_node_rows + node_grad_in[:, :features]
    grad_local = grad_local + jax.ops.segment_sum(edge_grad_in[:, 2 * features:], recv_all, num_segments=node_count)
    sender_grad = edge_grad_in[:, features:2 * features]
    weight_terms = (grad_edge_first, grad_edge_second, grad_node_first, grad_node_second)
    return (new_nodes, new_edges, grad_local, grad_edges, sender_grad, weight_terms)

def fine_senders(fine_send, sub_list, patch_list):
    base = (jnp.arange(DEVICES, dtype=jnp.int32) * NODE_DEV).reshape(N_PATCH, N_SUB)
    lists = sub_list.reshape(N_PATCH, N_SUB, N_SUB, HB)
    sub_rows = base[:, :, None, None] + lists
    sub_rows = jnp.transpose(sub_rows, (0, 2, 1, 3)).reshape(N_PATCH, N_SUB, N_SUB * HB)
    plists = patch_list.reshape(N_PATCH, N_SUB, 2, HB)
    upward = base[:, :, None] + plists[:, :, 0]
    downward = base[:, :, None] + plists[:, :, 1]
    from_lower = jnp.roll(upward, 1, axis=0)
    from_upper = jnp.roll(downward, -1, axis=0)
    own_rows = base[:, :, None] + jnp.arange(NODE_DEV, dtype=jnp.int32)[None, None, :]
    table = jnp.concatenate([own_rows, sub_rows, from_lower, from_upper], axis=2).reshape(DEVICES, EXT)
    return jnp.take_along_axis(table, fine_send.reshape(DEVICES, FINE_DEV).astype(jnp.int32), axis=1)

def reference(nodes, fine_edges, long_edges, fine_send, fine_recv, long_send, long_recv, long_mask, sub_list, patch_list, edge_w1, edge_w2, node_w1, node_w2, upstream_nodes, upstream_fine, upstream_long):
    features = nodes.shape[1]
    sender_fine = fine_senders(fine_send, sub_list, patch_list)
    sender_long = (long_send // COARSE_DEV * NODE_DEV + long_send % COARSE_DEV).astype(jnp.int32)
    sender_long = sender_long.reshape(DEVICES, LONG_CAP)

    def device_step(carry, items):
        table, sums = carry
        block, fine_rows, long_rows, send_fine, send_long, recv_fine, recv_long, mask_rows, up_nodes, up_fine, up_long = items
        senders = jnp.concatenate([send_fine, send_long])
        receivers = jnp.concatenate([recv_fine, recv_long])
        edge_in = jnp.concatenate([jnp.concatenate([fine_rows, long_rows], axis=0), jnp.take(nodes, senders, axis=0), jnp.take(block, receivers, axis=0)], axis=1)
        live_all = jnp.concatenate([jnp.ones((FINE_DEV, 1), jnp.float32), mask_rows.astype(jnp.float32)[:, None]], axis=0)
        upstream_edges = jnp.concatenate([up_fine, up_long], axis=0)
        result = layer_pass(block, edge_in, receivers, live_all, edge_w1, edge_w2, node_w1, node_w2, up_nodes, upstream_edges)
        table = table.at[senders].add(result[4])
        sums = tuple((total + term for total, term in zip(sums, result[5])))
        return ((table, sums), result[:4])
    items = (nodes.reshape(DEVICES, NODE_DEV, features), fine_edges.reshape(DEVICES, FINE_DEV, features), long_edges.reshape(DEVICES, LONG_CAP, features), sender_fine, sender_long, fine_recv.reshape(DEVICES, FINE_DEV).astype(jnp.int32), long_recv.reshape(DEVICES, LONG_CAP).astype(jnp.int32), long_mask.reshape(DEVICES, LONG_CAP), upstream_nodes.reshape(DEVICES, NODE_DEV, features), upstream_fine.reshape(DEVICES, FINE_DEV, features), upstream_long.reshape(DEVICES, LONG_CAP, features))
    start = (jnp.zeros((NODES, features), jnp.float32), (jnp.zeros((3 * features, features), jnp.float32), jnp.zeros((features, features), jnp.float32), jnp.zeros((2 * features, features), jnp.float32), jnp.zeros((features, features), jnp.float32)))
    (table, sums), stacked = lax.scan(device_step, start, items)
    new_blocks, new_edges, grad_local, grad_edges = stacked
    new_nodes = new_blocks.reshape(NODES, features)
    new_fine = new_edges[:, :FINE_DEV].reshape(FINE_E, features)
    new_long = new_edges[:, FINE_DEV:].reshape(LONG_E, features)
    grad_nodes = (grad_local.reshape(NODES, features) + table).astype(jnp.bfloat16)
    grad_fine = grad_edges[:, :FINE_DEV].reshape(FINE_E, features)
    grad_long = grad_edges[:, FINE_DEV:].reshape(LONG_E, features)
    return (new_nodes, new_fine, new_long, grad_nodes, grad_fine, grad_long, sums[0], sums[1], sums[2], sums[3])
```

```python
import functools
import math

import jax
import jax.numpy as jnp
from jax import lax
from jax.experimental import pallas as pl
from jax.experimental.pallas import tpu as pltpu
from jax.sharding import PartitionSpec as P

COARSE_DEV = 8
F32 = jnp.float32
BF16 = jnp.bfloat16
MESH = pl.DeviceIdType.MESH
EPS = 1e-05
TILE = 256
VMEM_BYTES = 56 * 1024 * 1024


def dot(left, right):
    return jnp.dot(left, right, preferred_element_type=F32)


def dot_tn(left, right):
    return lax.dot_general(left, right, (((0,), (0,)), ((), ())), preferred_element_type=F32)


def dot_nt(left, right):
    return lax.dot_general(left, right, (((1,), (1,)), ((), ())), preferred_element_type=F32)


def split(values):
    high = values.astype(BF16)
    return high, (values - high.astype(F32)).astype(BF16)


def marks(hits):
    return jnp.where(hits, 1.0, 0.0).astype(BF16)


class Place:
    def __init__(self, side, depth):
        self.p = lax.axis_index("patch")
        self.z = lax.axis_index("sub")
        self.side, self.depth = side, depth
        self.core = lax.rem(self.p, 2)
        self.x = lax.rem(lax.div(self.p, 2), side)
        self.y = lax.div(self.p, 2 * side)
        self.patches = 2 * side * side

    def at(self, y, x, core):
        return (y * self.side + x) * 2 + core

    def along_x(self, by):
        return (self.at(self.y, lax.rem(self.x + by, self.side), self.core), self.z)

    def along_y(self, by):
        return (self.at(lax.rem(self.y + by, self.side), self.x, self.core), self.z)

    def along_z(self, by):
        return (self.p, lax.rem(self.z + by, self.depth))

    def other_core(self):
        return (self.at(self.y, self.x, 1 - self.core), self.z)

    def next_patch(self):
        return (lax.rem(self.p + 1, self.patches), self.z)

    def previous_patch(self):
        return (lax.rem(self.p + self.patches - 1, self.patches), self.z)

    def greet(self):
        peers = [self.along_x(by) for by in range(1, self.side)]
        peers += [self.along_y(by) for by in range(1, self.side)]
        peers += [self.along_z(by) for by in range(1, self.depth)]
        peers += [self.other_core(), self.next_patch(), self.previous_patch()]
        barrier = pltpu.get_barrier_semaphore()
        for peer in peers:
            pl.semaphore_signal(barrier, inc=1, device_id=peer, device_id_type=MESH)
        pl.semaphore_wait(barrier, len(peers))


def send(source, target, sent, landed, peer):
    copy = pltpu.make_async_remote_copy(
        src_ref=source,
        dst_ref=target,
        send_sem=sent,
        recv_sem=landed,
        device_id=peer,
        device_id_type=MESH,
    )
    copy.start()
    return copy


def gather_kernel(
    side, depth, nodes, lists, ext, low, high, rows, sub_s, sub_r, pat_s, pat_r, z_s, z_r, a_s, a_r, b_s, b_r, c_s, c_r
):
    me = Place(side, depth)
    count, width = nodes.shape
    half = depth // 2
    hb = (lists.shape[1]) // (depth + 2)
    first = nodes[0:16, :].astype(F32)[0:8, :]
    block = jnp.concatenate([first[:, : width // 2], first[:, width // 2 :]], axis=0).astype(BF16)

    in_low = me.z < half
    z_low = lax.rem(me.z, half)

    @pl.when(in_low)
    def _():
        low[me.core, me.y, me.x, z_low] = block

    @pl.when(jnp.logical_not(in_low))
    def _():
        high[me.core, me.x, me.y, z_low] = block

    picks = marks(lax.broadcasted_iota(jnp.int32, (count, lists.shape[1]), 0) == lists[...])
    rows[...] = dot_tn(picks, nodes[...]).astype(BF16).reshape(depth + 2, hb, width)

    me.greet()

    def z_copy(by):
        mine_low = low.at[me.core, me.y, me.x, z_low]
        mine_high = high.at[me.core, me.x, me.y, z_low]
        peer = me.along_z(by)

        @pl.when(in_low)
        def _():
            send(mine_low, mine_low, z_s.at[by - 1], z_r.at[by - 1], peer)

        @pl.when(jnp.logical_not(in_low))
        def _():
            send(mine_high, mine_high, z_s.at[by - 1], z_r.at[by - 1], peer)

    for by in range(1, depth):
        z_copy(by)
    halo = []
    for by in range(1, depth):
        peer = me.along_z(by)
        target = ext.at[pl.ds(pl.multiple_of(count + hb * me.z, hb), hb), :]
        halo.append(send(rows.at[peer[1]], target, sub_s.at[by - 1], sub_r.at[by - 1], peer))
    lower = ext.at[pl.ds(count + hb * depth, hb), :]
    upper = ext.at[pl.ds(count + hb * (depth + 1), hb), :]
    halo.append(send(rows.at[depth], lower, pat_s.at[0], pat_r.at[0], me.next_patch()))
    halo.append(send(rows.at[depth + 1], upper, pat_s.at[1], pat_r.at[1], me.previous_patch()))
    ext[0:count, :] = nodes[...]
    ext[pl.ds(pl.multiple_of(count + hb * me.z, hb), hb), :] = rows[me.z]

    mine = low.at[0, 0, 0, 0]
    for by in range(1, depth):
        pltpu.make_async_remote_copy(
            src_ref=mine,
            dst_ref=mine,
            send_sem=z_s.at[by - 1],
            recv_sem=z_r.at[by - 1],
            device_id=me.along_z(by),
            device_id_type=MESH,
        ).wait()

    low_one = low.at[me.core, me.y, me.x]
    high_one = high.at[me.core, me.x, me.y]
    stage = []
    for by in range(1, side):
        stage.append(send(low_one, low_one, a_s.at[0, by - 1], a_r.at[0, by - 1], me.along_x(by)))
        stage.append(send(high_one, high_one, b_s.at[0, by - 1], b_r.at[0, by - 1], me.along_y(by)))
    for copy in stage:
        copy.wait()
    low_row = low.at[me.core, me.y]
    high_row = high.at[me.core, me.x]
    stage = []
    for by in range(1, side):
        stage.append(send(low_row, low_row, a_s.at[1, by - 1], a_r.at[1, by - 1], me.along_y(by)))
        stage.append(send(high_row, high_row, b_s.at[1, by - 1], b_r.at[1, by - 1], me.along_x(by)))
    for copy in stage:
        copy.wait()
    low_all, high_all = low.at[me.core], high.at[me.core]
    last = [
        send(low_all, low_all, c_s.at[0], c_r.at[0], me.other_core()),
        send(high_all, high_all, c_s.at[1], c_r.at[1], me.other_core()),
    ]
    for copy in halo + last:
        copy.wait()


def gather_rows(side, depth, nodes, lists):
    count, width = nodes.shape
    hb = lists.shape[1] // (depth + 2)
    half = depth // 2
    whole = pl.BlockSpec(memory_space=pltpu.VMEM)
    sem = pltpu.SemaphoreType.DMA
    table = jax.ShapeDtypeStruct((2, side, side, half, 16, width // 2), BF16)
    return pl.pallas_call(
        functools.partial(gather_kernel, side, depth),
        out_shape=(jax.ShapeDtypeStruct((count + lists.shape[1], width), BF16), table, table),
        in_specs=[whole] * 2,
        out_specs=(whole,) * 3,
        scratch_shapes=[
            pltpu.VMEM((depth + 2, hb, width), BF16),
            sem((depth - 1,)),
            sem((depth - 1,)),
            sem((2,)),
            sem((2,)),
            sem((depth - 1,)),
            sem((depth - 1,)),
            sem((2, side - 1)),
            sem((2, side - 1)),
            sem((2, side - 1)),
            sem((2, side - 1)),
            sem((2,)),
            sem((2,)),
        ],
        compiler_params=pltpu.CompilerParams(
            collective_id=0, has_side_effects=True, vmem_limit_bytes=VMEM_BYTES
        ),
        name="gather_rows",
    )(nodes, lists)


def norm_rows(values):
    centered = values - jnp.mean(values, axis=-1, keepdims=True)
    inverse = lax.rsqrt(jnp.mean(centered * centered, axis=-1, keepdims=True) + EPS)
    return centered * inverse, inverse


def norm_back(normed, inverse, upstream):
    mean_grad = jnp.mean(upstream, axis=-1, keepdims=True)
    mean_prod = jnp.mean(upstream * normed, axis=-1, keepdims=True)
    return (upstream - mean_grad - normed * mean_prod) * inverse


def silu_and_slope(values):
    sigma = 0.5 + 0.5 * jnp.tanh(0.5 * values)
    active = values * sigma
    return active, sigma + active * (1.0 - sigma)


def layer_kernel(
    side,
    depth,
    nodes,
    fine,
    longs,
    ext,
    low,
    high,
    idx,
    w1,
    w2,
    nw1,
    nw2,
    up_nodes,
    up_fine,
    up_long,
    new_nodes,
    new_fine,
    new_long,
    grad_fine,
    grad_long,
    table,
    halo,
    own,
    local,
    cols,
    slope,
    active,
    normed,
    inverse,
    senders,
    recv_proj,
    agg,
    ga,
    g1,
    g2,
    g_recv,
    g_ext,
    egf_long,
):
    count, width = nodes.shape
    fine_count = fine.shape[0]
    long_count = longs.shape[0]
    ext_rows = ext.shape[0]
    patches = 2 * side * side
    fine_tiles = fine_count // TILE
    long_tile = fine_count

    cols[...] = idx[...].T
    for ref in (agg, g1, g2, g_recv, g_ext):
        ref[...] = jnp.zeros_like(ref)

    high_part, low_part = split(dot(nodes[...], w1[2 * width : 3 * width, :]))
    recv_proj[0:count, :] = high_part
    recv_proj[count : 2 * count, :] = low_part

    def recv_cols(base):
        lanes = lax.broadcasted_iota(jnp.int32, (TILE, 2 * count), 1)
        return marks(lax.rem(lanes, count) == cols[pl.ds(base, TILE), 1:2])

    def recv_rows(base, live):
        rows = lax.broadcasted_iota(jnp.int32, (count, TILE), 0)
        hits = rows == idx[1:2, pl.ds(base, TILE)]
        if live:
            hits = jnp.logical_and(hits, idx[2:3, pl.ds(base, TILE)] > 0)
        return marks(hits)

    def forward(base, edges, sender, live):
        senders[pl.ds(base, TILE), :] = sender
        first = (
            dot(edges, w1[0:width, :])
            + dot(sender, w1[width : 2 * width, :])
            + dot(recv_cols(base), recv_proj[...])
        )
        act, slopes = silu_and_slope(first)
        act = act.astype(BF16)
        slope[pl.ds(base, TILE), :] = slopes
        active[pl.ds(base, TILE), :] = act
        unit, scale = norm_rows(dot(act, w2[...]))
        normed[pl.ds(base, TILE), :] = unit
        inverse[pl.ds(base, TILE), :] = jnp.broadcast_to(scale, (TILE, 128))
        if live is not None:
            unit = unit * live
        new = (edges.astype(F32) + unit).astype(BF16)
        agg[...] += dot(recv_rows(base, live is not None), new)
        return new

    def fine_forward(step, carry):
        base = pl.multiple_of(step * TILE, TILE)
        picks = marks(
            lax.broadcasted_iota(jnp.int32, (TILE, ext_rows), 1) == cols[pl.ds(base, TILE), 0:1]
        )
        sender = dot(picks, ext[...]).astype(BF16)
        new_fine[pl.ds(base, TILE), :] = forward(base, fine[pl.ds(base, TILE), :], sender, None)
        return carry

    lax.fori_loop(0, fine_tiles, fine_forward, 0)

    spot = cols[long_tile : long_tile + long_count, 0:1]
    major_rows = math.prod(low.shape[2:-1])
    lanes = lax.broadcasted_iota(jnp.int32, (long_count, major_rows), 1)
    left = jnp.zeros((long_count, width // 2), F32)
    right = jnp.zeros((long_count, width // 2), F32)
    for number in range(4 * side):
        part = low if number < 2 * side else high
        piece = part[number // side % 2, number % side].reshape(major_rows, width // 2)
        shifted = spot - number * major_rows
        left += dot(marks(lanes == shifted), piece)
        right += dot(marks(lanes == shifted + 8), piece)
    sender = jnp.concatenate([left, right], axis=1).astype(BF16)
    live = cols[long_tile : long_tile + long_count, 2:3].astype(F32)
    new_long[...] = forward(long_tile, longs[...], sender, live)

    node_rows = nodes[...]
    aggregate = agg[...].astype(BF16)
    node_first = dot(node_rows, nw1[0:width, :]) + dot(aggregate, nw1[width : 2 * width, :])
    node_active, node_slope = silu_and_slope(node_first)
    node_active = node_active.astype(BF16)
    node_normed, node_inverse = norm_rows(dot(node_active, nw2[...]))
    new_nodes[...] = (node_rows.astype(F32) + node_normed).astype(BF16)
    upstream = up_nodes[...].astype(F32)
    ngs = norm_back(node_normed, node_inverse, upstream).astype(BF16)
    ngf = (dot_nt(ngs, nw2[...]) * node_slope).astype(BF16)

    coarse_rows = COARSE_DEV * depth
    per = [w1.shape[0] // patches, w2.shape[0] // patches, nw1.shape[0] // patches, nw2.shape[0] // patches]
    starts = [coarse_rows, coarse_rows + per[0], coarse_rows + per[0] + per[1], coarse_rows + sum(per[:3])]

    def put(patch, start, values):
        core, x, y = patch % 2, patch // 2 % side, patch // (2 * side)
        values = values.astype(BF16)
        rows = pl.ds(start, values.shape[0])
        table[core, 0, x, y, rows, :] = values[:, : width // 2]
        table[core, 1, y, x, rows, :] = values[:, width // 2 :]

    def put_all(kind, values, first_patch, patch_count):
        for k in range(patch_count):
            put(first_patch + k, starts[kind], values[k * per[kind] : (k + 1) * per[kind], :])

    put_all(3, dot_tn(node_active, ngs), 0, patches)
    put_all(2, dot_tn(node_rows, ngf), 0, patches // 2)
    put_all(2, dot_tn(aggregate, ngf), patches // 2, patches // 2)
    local[...] = upstream + dot_nt(ngf, nw1[0:width, :])
    high_part, low_part = split(dot_nt(ngf, nw1[width : 2 * width, :]))
    ga[0:count, :] = high_part
    ga[count : 2 * count, :] = low_part

    def backward(base, edges, upstream_rows, live):
        pulled = dot(recv_cols(base), ga[...])
        if live is not None:
            pulled = pulled * live
        egn = upstream_rows.astype(F32) + pulled
        egs = norm_back(normed[pl.ds(base, TILE), :], inverse[pl.ds(base, TILE), 0:1], egn)
        if live is not None:
            egs = egs * live
        egs = egs.astype(BF16)
        egf = (dot_nt(egs, w2[...]) * slope[pl.ds(base, TILE), :]).astype(BF16)
        g2[...] += dot_tn(active[pl.ds(base, TILE), :], egs)
        g1[0:width, :] += dot_tn(edges, egf)
        g1[width : 2 * width, :] += dot_tn(senders[pl.ds(base, TILE), :], egf)
        g_recv[...] += dot(recv_rows(base, False), egf)
        return egf, (egn + dot_nt(egf, w1[0:width, :])).astype(BF16)

    def fine_backward(step, carry):
        base = pl.multiple_of(step * TILE, TILE)
        egf, grad = backward(base, fine[pl.ds(base, TILE), :], up_fine[pl.ds(base, TILE), :], None)
        grad_fine[pl.ds(base, TILE), :] = grad
        rows = lax.broadcasted_iota(jnp.int32, (ext_rows, TILE), 0)
        g_ext[...] += dot(marks(rows == idx[0:1, pl.ds(base, TILE)]), egf)
        return carry

    egf, grad = backward(long_tile, longs[...], up_long[...], live)
    grad_long[...] = grad
    egf_long[...] = egf
    lax.fori_loop(0, fine_tiles, fine_backward, 0)

    sources = idx[3:4, long_tile : long_tile + long_count]
    for patch in range(0, patches, 4):
        rows = lax.broadcasted_iota(jnp.int32, (4 * coarse_rows, long_count), 0) + patch * coarse_rows
        sums = dot(marks(rows == sources), egf_long[...])
        for k in range(4):
            put(patch + k, 0, sums[k * coarse_rows : (k + 1) * coarse_rows, :])

    high_part, low_part = split(g_recv[...])
    g1[2 * width : 3 * width, :] = dot_tn(node_rows, high_part) + dot_tn(node_rows, low_part)
    receiver_w = w1[2 * width : 3 * width, :]
    local[...] += dot_nt(high_part, receiver_w) + dot_nt(low_part, receiver_w)
    for patch in range(patches):
        put(patch, starts[0], g1[patch * per[0] : (patch + 1) * per[0], :])
        put(patch, starts[1], g2[patch * per[1] : (patch + 1) * per[1], :])
    own[...] = g_ext[0:count, :]
    halo[...] = g_ext[count:ext_rows, :].astype(BF16)


def layer(side, depth, nodes, fine, longs, ext, low, high, idx, w1, w2, nw1, nw2, up_nodes, up_fine, up_long):
    count, width = nodes.shape
    edges = fine.shape[0] + longs.shape[0]
    patches = 2 * side * side
    chunk = COARSE_DEV * depth + (w1.shape[0] + w2.shape[0] + nw1.shape[0] + nw2.shape[0]) // patches
    whole = pl.BlockSpec(memory_space=pltpu.VMEM)

    def like(array):
        return jax.ShapeDtypeStruct(array.shape, array.dtype)

    def shape(dims, kind):
        return jax.ShapeDtypeStruct(dims, kind)

    return pl.pallas_call(
        functools.partial(layer_kernel, side, depth),
        out_shape=(
            like(nodes),
            like(fine),
            like(longs),
            like(fine),
            like(longs),
            shape((2, 2, side, side, chunk, width // 2), BF16),
            shape((ext.shape[0] - count, width), BF16),
            shape((count, width), F32),
            shape((count, width), F32),
        ),
        in_specs=[whole] * 14,
        out_specs=(whole,) * 9,
        scratch_shapes=[
            pltpu.VMEM((edges, idx.shape[0]), jnp.int32),
            pltpu.VMEM((edges, width), F32),
            pltpu.VMEM((edges, width), BF16),
            pltpu.VMEM((edges, width), F32),
            pltpu.VMEM((edges, 128), F32),
            pltpu.VMEM((edges, width), BF16),
            pltpu.VMEM((2 * count, width), BF16),
            pltpu.VMEM((count, width), F32),
            pltpu.VMEM((2 * count, width), BF16),
            pltpu.VMEM(w1.shape, F32),
            pltpu.VMEM(w2.shape, F32),
            pltpu.VMEM((count, width), F32),
            pltpu.VMEM((ext.shape[0], width), F32),
            pltpu.VMEM((longs.shape[0], width), BF16),
        ],
        compiler_params=pltpu.CompilerParams(vmem_limit_bytes=VMEM_BYTES),
        name="layer",
    )(nodes, fine, longs, ext, low, high, idx, w1, w2, nw1, nw2, up_nodes, up_fine, up_long)


def reduce_kernel(
    side,
    depth,
    table,
    halo,
    own,
    local,
    lists,
    w1,
    out_a,
    out_b,
    out_c,
    out_d,
    grad_nodes,
    mine,
    other,
    first_in,
    second,
    second_in,
    z_out,
    z_in,
    shares,
    back,
    local_sem,
    core_s,
    core_r,
    x_s,
    x_r,
    y_s,
    y_r,
    z_s,
    z_r,
    w_s,
    w_r,
    sub_s,
    sub_r,
    pat_s,
    pat_r,
):
    me = Place(side, depth)
    count, width = own.shape
    half = width // 2
    hb = lists.shape[1] // (depth + 2)
    coarse_rows = COARSE_DEV * depth
    chunk = table.shape[4]
    share = (z_out.shape[1] - 16) // 2
    order = [2, 1, 3, 0] if side == 4 else list(range(1, side)) + [0]
    majors = (me.x, me.y)
    minors = (me.y, me.x)

    locals_ = {}
    for by in order:
        for part in (0, 1):
            major = lax.rem(majors[part] + by, side)
            copy = pltpu.make_async_copy(
                table.at[me.core, part, major], mine.at[part, major], local_sem.at[part, by]
            )
            copy.start()
            locals_[part, by] = copy

    me.greet()

    cores = {}
    for by in order:
        for part in (0, 1):
            major = lax.rem(majors[part] + by, side)
            cores[part, by] = send(
                table.at[1 - me.core, part, major],
                other.at[part, major],
                core_s.at[part, by],
                core_r.at[part, by],
                me.other_core(),
            )

    returns = []
    for by in range(1, depth):
        peer = me.along_z(by)
        source = halo.at[pl.ds(pl.multiple_of(hb * peer[1], hb), hb), :]
        returns.append(send(source, back.at[me.z], sub_s.at[by - 1], sub_r.at[by - 1], peer))
    lower = halo.at[pl.ds(hb * depth, hb), :]
    upper = halo.at[pl.ds(hb * (depth + 1), hb), :]
    returns.append(send(lower, back.at[depth], pat_s.at[0], pat_r.at[0], me.previous_patch()))
    returns.append(send(upper, back.at[depth + 1], pat_s.at[1], pat_r.at[1], me.next_patch()))
    back[me.z] = halo[pl.ds(pl.multiple_of(hb * me.z, hb), hb), :]

    firsts = {}
    for by in order:
        for part in (0, 1):
            major = lax.rem(majors[part] + by, side)
            locals_[part, by].wait()
            cores[part, by].wait_recv()

            def add(minor, carry, part=part, major=major):
                mine[part, major, minor] = mine[part, major, minor] + other[part, major, minor]
                return carry

            lax.fori_loop(0, side, add, 0)
            if by:
                peer = me.along_x(by) if part == 0 else me.along_y(by)
                firsts[part, by] = send(
                    mine.at[part, major],
                    first_in.at[part, by - 1],
                    x_s.at[part, by - 1],
                    x_r.at[part, by - 1],
                    peer,
                )

    for copy in returns:
        copy.wait()
    picks = marks(lax.broadcasted_iota(jnp.int32, (count, lists.shape[1]), 0) == lists[...])
    sent = own[...] + dot(picks, back[...].reshape((depth + 2) * hb, width))

    for key in firsts:
        firsts[key].wait_recv()
    seconds = {}
    for by in order:
        for part in (0, 1):
            minor = lax.rem(minors[part] + by, side)
            total = mine[part, majors[part], minor].astype(F32)
            for k in range(side - 1):
                total = total + first_in[part, k, minor].astype(F32)
            second[part, minor] = total.astype(BF16)
            if by:
                peer = me.along_y(by) if part == 0 else me.along_x(by)
                seconds[part, by] = send(
                    second.at[part, minor],
                    second_in.at[part, by - 1],
                    y_s.at[part, by - 1],
                    y_r.at[part, by - 1],
                    peer,
                )
    sums = []
    for part in (0, 1):
        for by in range(1, side):
            seconds[part, by].wait_recv()
        total = second[part, minors[part]].astype(F32)
        for k in range(side - 1):
            total = total + second_in[part, k].astype(F32)
        sums.append(total)

    blocks = (chunk - coarse_rows) // 16
    for k in range(depth):
        rows = slice(k * COARSE_DEV, (k + 1) * COARSE_DEV)
        z_out[k, 0:16, :] = jnp.concatenate([sums[0][rows, :], sums[1][rows, :]], axis=0).astype(BF16)
        for j in range(share // 16):
            at = k * (share // 16) + j
            for part in (0, 1):
                target = pl.ds(16 + part * share + 16 * j, 16)
                if at < blocks:
                    start = coarse_rows + 16 * at
                    z_out[k, target, :] = sums[part][start : start + 16, :].astype(BF16)
                else:
                    z_out[k, target, :] = jnp.zeros((16, half), BF16)
    zs = []
    for by in range(1, depth):
        peer = me.along_z(by)
        zs.append(send(z_out.at[peer[1]], z_in.at[by - 1], z_s.at[by - 1], z_r.at[by - 1], peer))
    for copy in zs:
        copy.wait_recv()
    total = z_out[me.z].astype(F32)
    for k in range(depth - 1):
        total = total + z_in[k].astype(F32)
    shares[me.z] = total[16:, :].astype(BF16)
    ws = []
    for by in range(1, depth):
        ws.append(send(shares.at[me.z], shares.at[me.z], w_s.at[by - 1], w_r.at[by - 1], me.along_z(by)))

    coarse = jnp.concatenate([total[0:8, :], total[8:16, :]], axis=1)
    sent = jnp.concatenate([sent[0:8, :] + coarse, sent[8:, :]], axis=0)
    high_part, low_part = split(sent)
    sender_w = w1[width : 2 * width, :]
    grad_nodes[...] = (local[...] + dot_nt(high_part, sender_w) + dot_nt(low_part, sender_w)).astype(BF16)

    for copy in ws:
        copy.wait_recv()
    at = 0
    for out in (out_a, out_b, out_c, out_d):
        for row in range(0, out.shape[0], 16):
            k, j = at // (share // 16), at % (share // 16)
            for part in (0, 1):
                piece = shares[k, part * share + 16 * j : part * share + 16 * (j + 1), :]
                out[row : row + 16, part * half : (part + 1) * half] = piece.astype(F32)
            at += 1
    for key in cores:
        cores[key].wait_send()
    for key in firsts:
        firsts[key].wait_send()
    for key in seconds:
        seconds[key].wait_send()
    for copy in zs + ws:
        copy.wait_send()


def reduce_all(side, depth, table, halo, own, local, lists, w1, sizes):
    count, width = own.shape
    half = width // 2
    hb = lists.shape[1] // (depth + 2)
    chunk = table.shape[4]
    blocks = (chunk - COARSE_DEV * depth) // 16
    share = 16 * -(-blocks // depth)
    whole = pl.BlockSpec(memory_space=pltpu.VMEM)
    sem = pltpu.SemaphoreType.DMA
    return pl.pallas_call(
        functools.partial(reduce_kernel, side, depth),
        out_shape=tuple(jax.ShapeDtypeStruct((rows, width), F32) for rows in sizes)
        + (jax.ShapeDtypeStruct((count, width), BF16),),
        in_specs=[pl.BlockSpec(memory_space=pl.ANY)] + [whole] * 5,
        out_specs=(whole,) * 5,
        scratch_shapes=[
            pltpu.VMEM((2, side, side, chunk, half), BF16),
            pltpu.VMEM((2, side, side, chunk, half), BF16),
            pltpu.VMEM((2, side - 1, side, chunk, half), BF16),
            pltpu.VMEM((2, side, chunk, half), BF16),
            pltpu.VMEM((2, side - 1, chunk, half), BF16),
            pltpu.VMEM((depth, 16 + 2 * share, half), BF16),
            pltpu.VMEM((depth - 1, 16 + 2 * share, half), BF16),
            pltpu.VMEM((depth, 2 * share, half), BF16),
            pltpu.VMEM((depth + 2, hb, width), BF16),
            sem((2, side)),
            sem((2, side)),
            sem((2, side)),
            sem((2, side - 1)),
            sem((2, side - 1)),
            sem((2, side - 1)),
            sem((2, side - 1)),
            sem((depth - 1,)),
            sem((depth - 1,)),
            sem((depth - 1,)),
            sem((depth - 1,)),
            sem((depth - 1,)),
            sem((depth - 1,)),
            sem((2,)),
            sem((2,)),
        ],
        compiler_params=pltpu.CompilerParams(
            collective_id=1, has_side_effects=True, vmem_limit_bytes=VMEM_BYTES
        ),
        name="reduce_all",
    )(table, halo, own, local, lists, w1)


def coarse_spot(side, depth, coarse):
    block, row = coarse // COARSE_DEV, coarse % COARSE_DEV
    patch, z = block // depth, block % depth
    core, x, y = patch % 2, patch // 2 % side, patch // (2 * side)
    half = depth // 2
    lower = z < half
    major, minor = jnp.where(lower, y, x), jnp.where(lower, x, y)
    place = ((core * side + major) * side + minor) * half + z % half
    return 16 * (place + jnp.where(lower, 0, 2 * side * side * half)) + row


def per_device(
    side,
    depth,
    nodes,
    fine_edges,
    long_edges,
    fine_send,
    fine_recv,
    long_send,
    long_recv,
    long_mask,
    sub_list,
    patch_list,
    edge_w1,
    edge_w2,
    node_w1,
    node_w2,
    upstream_nodes,
    upstream_fine,
    upstream_long,
):
    patches = 2 * side * side
    lists = jnp.concatenate([sub_list.reshape(1, -1), patch_list.reshape(1, -1)], axis=1)
    ones = jnp.ones_like(fine_send)
    none = jnp.zeros_like(fine_send)
    idx = jnp.stack(
        [
            jnp.concatenate([fine_send, coarse_spot(side, depth, long_send)]),
            jnp.concatenate([fine_recv, long_recv]),
            jnp.concatenate([ones, long_mask]),
            jnp.concatenate([none, long_send]),
        ]
    )
    idx = jnp.concatenate([idx, jnp.zeros_like(idx)], axis=0)
    ext, low, high = gather_rows(side, depth, nodes, lists)
    new_nodes, new_fine, new_long, grad_fine, grad_long, table, halo, own, local = layer(
        side,
        depth,
        nodes,
        fine_edges,
        long_edges,
        ext,
        low,
        high,
        idx,
        edge_w1,
        edge_w2,
        node_w1,
        node_w2,
        upstream_nodes,
        upstream_fine,
        upstream_long,
    )
    sizes = [w.shape[0] // patches for w in (edge_w1, edge_w2, node_w1, node_w2)]
    totals = reduce_all(side, depth, table, halo, own, local, lists, edge_w1, sizes)
    return (new_nodes, new_fine, new_long, totals[4], grad_fine, grad_long) + tuple(totals[:4])


def solution(mesh):
    side = math.isqrt(mesh.shape["patch"] // 2)
    depth = mesh.shape["sub"]
    rows = P(("patch", "sub"), None)
    flat = P(("patch", "sub"))
    return jax.shard_map(
        functools.partial(per_device, side, depth),
        mesh=mesh,
        in_specs=(rows,) * 3 + (flat,) * 5 + (rows,) * 2 + (P(),) * 4 + (rows,) * 3,
        out_specs=(rows,) * 6 + (P("patch", None),) * 4,
        check_vma=False,
    )
```

```python
import functools
import math
from types import SimpleNamespace

import jax
import jax.numpy as jnp
from jax import lax
from jax.experimental import pallas as pl
from jax.experimental.pallas import tpu as pltpu
from jax.sharding import PartitionSpec as P

COARSE_DEV = 8
F32 = jnp.float32
BF16 = jnp.bfloat16
MESH = pl.DeviceIdType.MESH
EPS = 1e-05
TILE = 256
VMEM_BYTES = 56 * 1024 * 1024


def dot(left, right):
    return jnp.dot(left, right, preferred_element_type=F32)


def dot_tn(left, right):
    return lax.dot_general(left, right, (((0,), (0,)), ((), ())), preferred_element_type=F32)


def dot_nt(left, right):
    return lax.dot_general(left, right, (((1,), (1,)), ((), ())), preferred_element_type=F32)


def split(values):
    high = values.astype(BF16)
    return high, (values - high.astype(F32)).astype(BF16)


def marks(hits):
    return jnp.where(hits, 1.0, 0.0).astype(BF16)


class Place:
    def __init__(self, side, depth):
        self.p = lax.axis_index("patch")
        self.z = lax.axis_index("sub")
        self.side, self.depth = side, depth
        self.core = lax.rem(self.p, 2)
        self.x = lax.rem(lax.div(self.p, 2), side)
        self.y = lax.div(self.p, 2 * side)
        self.patches = 2 * side * side

    def at(self, y, x, core):
        return (y * self.side + x) * 2 + core

    def along_x(self, by):
        return (self.at(self.y, lax.rem(self.x + by, self.side), self.core), self.z)

    def along_y(self, by):
        return (self.at(lax.rem(self.y + by, self.side), self.x, self.core), self.z)

    def along_z(self, by):
        return (self.p, lax.rem(self.z + by, self.depth))

    def other_core(self):
        return (self.at(self.y, self.x, 1 - self.core), self.z)

    def next_patch(self):
        return (lax.rem(self.p + 1, self.patches), self.z)

    def previous_patch(self):
        return (lax.rem(self.p + self.patches - 1, self.patches), self.z)

    def greet(self):
        peers = [self.along_x(by) for by in range(1, self.side)]
        peers += [self.along_y(by) for by in range(1, self.side)]
        peers += [self.along_z(by) for by in range(1, self.depth)]
        peers += [self.other_core(), self.next_patch(), self.previous_patch()]
        barrier = pltpu.get_barrier_semaphore()
        for peer in peers:
            pl.semaphore_signal(barrier, inc=1, device_id=peer, device_id_type=MESH)
        pl.semaphore_wait(barrier, len(peers))


def remote(source, target, sent, landed, peer):
    return pltpu.make_async_remote_copy(
        src_ref=source,
        dst_ref=target,
        send_sem=sent,
        recv_sem=landed,
        device_id=peer,
        device_id_type=MESH,
    )


def send(source, target, sent, landed, peer):
    copy = remote(source, target, sent, landed, peer)
    copy.start()
    return copy


def norm_rows(values):
    centered = values - jnp.mean(values, axis=-1, keepdims=True)
    inverse = lax.rsqrt(jnp.mean(centered * centered, axis=-1, keepdims=True) + EPS)
    return centered * inverse, inverse


def norm_back(normed, inverse, upstream):
    mean_grad = jnp.mean(upstream, axis=-1, keepdims=True)
    mean_prod = jnp.mean(upstream * normed, axis=-1, keepdims=True)
    return (upstream - mean_grad - normed * mean_prod) * inverse


def silu_and_slope(values):
    sigma = 0.5 + 0.5 * jnp.tanh(0.5 * values)
    active = values * sigma
    return active, sigma + active * (1.0 - sigma)


def coarse_spot(side, depth, coarse):
    block, row = coarse // COARSE_DEV, coarse % COARSE_DEV
    patch, z = block // depth, block % depth
    core, x, y = patch % 2, patch // 2 % side, patch // (2 * side)
    half = depth // 2
    lower = z < half
    major, minor = jnp.where(lower, y, x), jnp.where(lower, x, y)
    place = ((core * side + major) * side + minor) * half + z % half
    return 16 * (place + jnp.where(lower, 0, 2 * side * side * half)) + row


class Sum:
    def __init__(self, me, refs, name):
        self.me, self.side = me, me.side
        for key, ref in vars(refs).items():
            if key.startswith(name + "_"):
                setattr(self, key[len(name) + 1 :], ref)
        self.majors, self.minors = (me.x, me.y), (me.y, me.x)

    def put(self, patch, start, values):
        side, half = self.side, self.table.shape[-1]
        core, x, y = patch % 2, patch // 2 % side, patch // (2 * side)
        values = values.astype(BF16)
        rows = pl.ds(start, values.shape[0])
        self.table[core, 0, x, y, rows, :] = values[:, :half]
        self.table[core, 1, y, x, rows, :] = values[:, half:]

    def put_all(self, start, values, patches, first=0):
        per = values.shape[0] // patches
        for k in range(patches):
            self.put(first + k, start, values[k * per : (k + 1) * per, :])

    def start(self):
        self.cores = []
        for part in (0, 1):
            source, target = self.table.at[1 - self.me.core, part], self.other.at[part]
            sems = self.core_sem.at[0, part], self.core_sem.at[1, part]
            self.cores.append(send(source, target, *sems, self.me.other_core()))

    def first(self):
        me, side = self.me, self.side
        self.firsts = []
        for copy in self.cores:
            copy.wait_recv()
        for by in [*range(1, side), 0]:
            for part in (0, 1):
                major = lax.rem(self.majors[part] + by, side)

                def add(minor, carry, part=part, major=major):
                    spot = (me.core, part, major, minor)
                    self.table[spot] = self.table[spot] + self.other[part, major, minor]
                    return carry

                lax.fori_loop(0, side, add, 0)
                if by:
                    peer = me.along_x(by) if part == 0 else me.along_y(by)
                    source, target = self.table.at[me.core, part, major], self.first_in.at[part, by - 1]
                    sems = self.first_sem.at[0, part, by - 1], self.first_sem.at[1, part, by - 1]
                    self.firsts.append(send(source, target, *sems, peer))

    def second(self):
        me, side = self.me, self.side
        self.seconds = []
        for copy in self.firsts:
            copy.wait_recv()
        for by in [*range(1, side), 0]:
            for part in (0, 1):
                minor = lax.rem(self.minors[part] + by, side)
                total = self.table[me.core, part, self.majors[part], minor].astype(F32)
                for k in range(side - 1):
                    total = total + self.first_in[part, k, minor].astype(F32)
                self.middle[part, minor] = total.astype(BF16)
                if by:
                    peer = me.along_y(by) if part == 0 else me.along_x(by)
                    source, target = self.middle.at[part, minor], self.second_in.at[part, by - 1]
                    sems = self.second_sem.at[0, part, by - 1], self.second_sem.at[1, part, by - 1]
                    self.seconds.append(send(source, target, *sems, peer))

    def patch_total(self):
        for copy in self.seconds:
            copy.wait_recv()
        sums = []
        for part in (0, 1):
            total = self.middle[part, self.minors[part]].astype(F32)
            for k in range(self.side - 1):
                total = total + self.second_in[part, k].astype(F32)
            sums.append(total)
        return sums

    def across(self, blocks):
        me, depth = self.me, self.me.depth
        per = self.z_out.shape[1]
        for k in range(depth * per):
            if k < len(blocks):
                self.z_out[k // per, k % per] = blocks[k].astype(BF16)
            else:
                self.z_out[k // per, k % per] = jnp.zeros(self.z_out.shape[2:], BF16)
        self.crossing = []
        for by in range(1, depth):
            peer = me.along_z(by)
            sems = self.z_sem.at[0, by - 1], self.z_sem.at[1, by - 1]
            self.crossing.append(send(self.z_out.at[peer[1]], self.z_in.at[by - 1], *sems, peer))

    def cross_total(self):
        for copy in self.crossing:
            copy.wait_recv()
        total = self.z_out[self.me.z].astype(F32)
        for k in range(self.me.depth - 1):
            total = total + self.z_in[k].astype(F32)
        return total

    def share(self, total):
        me = self.me
        self.shares[me.z] = total.astype(BF16)
        self.sharing = []
        for by in range(1, me.depth):
            mine = self.shares.at[me.z]
            sems = self.w_sem.at[0, by - 1], self.w_sem.at[1, by - 1]
            self.sharing.append(send(mine, mine, *sems, me.along_z(by)))

    def block(self, k):
        per = self.shares.shape[1]
        return self.shares[k // per, k % per].astype(F32)

    def wait_sends(self):
        for copy in self.cores + self.firsts + self.seconds + self.crossing + self.sharing:
            copy.wait_send()

    sharing = []


def sum_scratch(side, depth, rows, half, blocks):
    per = -(-blocks // depth)
    sem = pltpu.SemaphoreType.DMA
    return dict(
        table=pltpu.VMEM((2, 2, side, side, rows, half), BF16),
        other=pltpu.VMEM((2, side, side, rows, half), BF16),
        first_in=pltpu.VMEM((2, side - 1, side, rows, half), BF16),
        middle=pltpu.VMEM((2, side, rows, half), BF16),
        second_in=pltpu.VMEM((2, side - 1, rows, half), BF16),
        z_out=pltpu.VMEM((depth, per, 16, half), BF16),
        z_in=pltpu.VMEM((depth - 1, per, 16, half), BF16),
        shares=pltpu.VMEM((depth, per, 16, half), BF16),
        core_sem=sem((2, 2)),
        first_sem=sem((2, 2, side - 1)),
        second_sem=sem((2, 2, side - 1)),
        z_sem=sem((2, depth - 1)),
        w_sem=sem((2, depth - 1)),
    )


def row_blocks(sums):
    return [part[at : at + 16, :] for at in range(0, sums[0].shape[0], 16) for part in sums]


def whole_kernel(side, depth, names, loaded, *all_refs):
    refs = SimpleNamespace(**dict(zip(names, all_refs)))
    me = Place(side, depth)
    nodes, ext, low, high, rows = refs.nodes, refs.ext, refs.low, refs.high, refs.rows
    idx, cols, lists = refs.idx, refs.cols, refs.lists
    count, width = nodes.shape
    half = depth // 2
    columns = width // 2
    hb = refs.sub_list.shape[1]
    fine_count = refs.fine.shape[0]
    long_count = refs.longs.shape[0]
    ext_rows = ext.shape[0]
    patches = 2 * side * side
    fine_tiles = fine_count // TILE
    long_tile = fine_count

    loads = SimpleNamespace()
    for number, name in enumerate(loaded):
        local_copy = getattr(refs, "v_" + name)
        copy = pltpu.make_async_copy(getattr(refs, name), local_copy, refs.load_sem.at[number])
        copy.start()
        setattr(loads, name, copy)
    w1, w2, nw1, nw2 = refs.v_w1, refs.v_w2, refs.v_nw1, refs.v_nw2
    fine, longs, up_fine, up_long = refs.v_fine, refs.v_longs, refs.v_up_fine, refs.v_up_long

    first = nodes[0:16, :].astype(F32)[0:8, :]
    block = jnp.concatenate([first[:, :columns], first[:, columns:]], axis=0).astype(BF16)
    in_low = me.z < half
    z_low = lax.rem(me.z, half)

    @pl.when(in_low)
    def _():
        low[me.core, me.y, me.x, z_low] = block

    @pl.when(jnp.logical_not(in_low))
    def _():
        high[me.core, me.x, me.y, z_low] = block

    for k in range(depth):
        lists[0:1, k * hb : (k + 1) * hb] = refs.sub_list[k : k + 1, :]
    for k in range(2):
        lists[0:1, (depth + k) * hb : (depth + k + 1) * hb] = refs.patch_list[k : k + 1, :]
    picks = marks(lax.broadcasted_iota(jnp.int32, (count, lists.shape[1]), 0) == lists[...])
    rows[...] = dot_tn(picks, nodes[...]).astype(BF16).reshape(depth + 2, hb, width)

    me.greet()

    for by in range(1, depth):
        sems = refs.zs_sem.at[0, by - 1], refs.zs_sem.at[1, by - 1]

        @pl.when(in_low)
        def _():
            mine = low.at[me.core, me.y, me.x, z_low]
            send(mine, mine, *sems, me.along_z(by))

        @pl.when(jnp.logical_not(in_low))
        def _():
            mine = high.at[me.core, me.x, me.y, z_low]
            send(mine, mine, *sems, me.along_z(by))

    halo = []
    own_rows = pl.ds(pl.multiple_of(count + hb * me.z, hb), hb)
    for by in range(1, depth):
        peer = me.along_z(by)
        sems = refs.sub_sem.at[0, by - 1], refs.sub_sem.at[1, by - 1]
        halo.append(send(rows.at[peer[1]], ext.at[own_rows, :], *sems, peer))
    for k, peer in enumerate((me.next_patch(), me.previous_patch())):
        target = ext.at[pl.ds(count + hb * (depth + k), hb), :]
        sems = refs.pat_sem.at[0, k], refs.pat_sem.at[1, k]
        halo.append(send(rows.at[depth + k], target, *sems, peer))

    idx[...] = jnp.zeros_like(idx)
    spots = coarse_spot(side, depth, refs.long_send[...])
    for k in range(fine_count // 128):
        lanes = slice(128 * k, 128 * (k + 1))
        idx[0:1, lanes] = refs.fine_send[k : k + 1, :]
        idx[1:2, lanes] = refs.fine_recv[k : k + 1, :]
    for k in range(long_count // 128):
        lanes = slice(fine_count + 128 * k, fine_count + 128 * (k + 1))
        idx[0:1, lanes] = spots[k : k + 1, :]
        idx[1:2, lanes] = refs.long_recv[k : k + 1, :]
        idx[2:3, lanes] = refs.long_mask[k : k + 1, :]
        idx[3:4, lanes] = refs.long_send[k : k + 1, :]
    cols[...] = idx[...].T
    ext[0:count, :] = nodes[...]
    ext[own_rows, :] = rows[me.z]
    agg, ga, g1, g2 = refs.agg, refs.ga, refs.g1, refs.g2
    g_recv, g_ext, recv_proj = refs.g_recv, refs.g_ext, refs.recv_proj
    for ref in (agg, g1, g2, g_recv, g_ext):
        ref[...] = jnp.zeros_like(ref)

    loads.w1.wait()
    high_part, low_part = split(dot(nodes[...], w1[2 * width : 3 * width, :]))
    recv_proj[0:count, :] = high_part
    recv_proj[count : 2 * count, :] = low_part

    mine = low.at[0, 0, 0, 0]
    for by in range(1, depth):
        sems = refs.zs_sem.at[0, by - 1], refs.zs_sem.at[1, by - 1]
        remote(mine, mine, *sems, me.along_z(by)).wait()

    def spread(step, low_part, high_part):
        copies = []
        for by in range(1, side):
            along = (me.along_x(by), me.along_y(by))
            for k, part in enumerate((low_part, high_part)):
                sems = refs.ab_sem.at[0, step, k, by - 1], refs.ab_sem.at[1, step, k, by - 1]
                copies.append(send(part, part, *sems, along[(step + k) % 2]))
        return copies

    spreading = spread(0, low.at[me.core, me.y, me.x], high.at[me.core, me.x, me.y])

    slope, active, normed, inverse = refs.slope, refs.active, refs.normed, refs.inverse
    senders = refs.senders

    def recv_cols(base):
        lanes = lax.broadcasted_iota(jnp.int32, (TILE, 2 * count), 1)
        return marks(lax.rem(lanes, count) == cols[base : base + TILE, 1:2])

    def recv_rows(base, live):
        spots = lax.broadcasted_iota(jnp.int32, (count, TILE), 0)
        hits = spots == idx[1:2, base : base + TILE]
        if live:
            hits = jnp.logical_and(hits, idx[2:3, base : base + TILE] > 0)
        return marks(hits)

    def forward(base, edges, sender, rest, live):
        senders[base : base + TILE, :] = sender
        act, slopes = silu_and_slope(rest + dot(sender, w1[width : 2 * width, :]))
        act = act.astype(BF16)
        slope[base : base + TILE, :] = slopes
        active[base : base + TILE, :] = act
        unit, scale = norm_rows(dot(act, w2[...]))
        normed[base : base + TILE, :] = unit
        inverse[base : base + TILE, :] = jnp.broadcast_to(scale, (TILE, 128))
        if live is not None:
            unit = unit * live
        new = (edges.astype(F32) + unit).astype(BF16)
        agg[...] += dot(recv_rows(base, live is not None), new)
        return new

    def sender_free(base, edges):
        return dot(edges, w1[0:width, :]) + dot(recv_cols(base), recv_proj[...])

    loads.fine.wait()
    loads.w2.wait()
    for copy in halo:
        copy.wait_recv()
    for step in range(fine_tiles):
        base = step * TILE
        edges = fine[base : base + TILE, :]
        lanes = lax.broadcasted_iota(jnp.int32, (TILE, ext_rows), 1)
        picks = marks(lanes == cols[base : base + TILE, 0:1])
        sender = dot(picks, ext[...]).astype(BF16)
        refs.v_new_fine[base : base + TILE, :] = forward(
            base, edges, sender, sender_free(base, edges), None
        )
        if step == 0:
            for copy in spreading:
                copy.wait()
            spreading = spread(1, low.at[me.core, me.y], high.at[me.core, me.x])
    loads.longs.wait()
    edges = longs[...]
    rest = sender_free(long_tile, edges)
    for copy in spreading:
        copy.wait()
    spreading = []
    for k, part in enumerate((low.at[me.core], high.at[me.core])):
        sems = refs.cc_sem.at[0, k], refs.cc_sem.at[1, k]
        spreading.append(send(part, part, *sems, me.other_core()))
    for copy in spreading:
        copy.wait()

    spot = cols[long_tile : long_tile + long_count, 0:1]
    major_rows = math.prod(low.shape[2:-1])
    lanes = lax.broadcasted_iota(jnp.int32, (long_count, major_rows), 1)
    left = jnp.zeros((long_count, columns), F32)
    right = jnp.zeros((long_count, columns), F32)
    for number in range(4 * side):
        part = low if number < 2 * side else high
        piece = part[number // side % 2, number % side].reshape(major_rows, columns)
        shifted = spot - number * major_rows
        left += dot(marks(lanes == shifted), piece)
        right += dot(marks(lanes == shifted + 8), piece)
    sender = jnp.concatenate([left, right], axis=1).astype(BF16)
    live = cols[long_tile : long_tile + long_count, 2:3].astype(F32)
    refs.v_new_long[...] = forward(long_tile, edges, sender, rest, live)

    stores = []

    def store(source, target):
        copy = pltpu.make_async_copy(source, target, refs.store_sem.at[len(stores)])
        copy.start()
        stores.append(copy)

    store(refs.v_new_fine, refs.out_fine)
    store(refs.v_new_long, refs.out_long)

    loads.nw1.wait()
    loads.nw2.wait()
    loads.up_nodes.wait()
    node_rows = nodes[...]
    aggregate = agg[...].astype(BF16)
    node_first = dot(node_rows, nw1[0:width, :]) + dot(aggregate, nw1[width : 2 * width, :])
    node_active, node_slope = silu_and_slope(node_first)
    node_active = node_active.astype(BF16)
    node_normed, node_inverse = norm_rows(dot(node_active, nw2[...]))
    refs.out_node[...] = (node_rows.astype(F32) + node_normed).astype(BF16)
    upstream = refs.v_up_nodes[...].astype(F32)
    ngs = norm_back(node_normed, node_inverse, upstream).astype(BF16)
    ngf = (dot_nt(ngs, nw2[...]) * node_slope).astype(BF16)
    by_node = Sum(me, refs, "n")
    per = [ref.shape[0] // patches for ref in (w1, w2, nw1, nw2)]
    by_node.put_all(per[2], dot_tn(node_active, ngs), patches)
    by_node.put_all(0, dot_tn(node_rows, ngf), patches // 2)
    by_node.put_all(0, dot_tn(aggregate, ngf), patches // 2, patches // 2)
    by_node.start()
    local = refs.local
    local[...] = upstream + dot_nt(ngf, nw1[0:width, :])
    high_part, low_part = split(dot_nt(ngf, nw1[width : 2 * width, :]))
    ga[0:count, :] = high_part
    ga[count : 2 * count, :] = low_part

    def backward(base, edges, upstream_rows, live):
        pulled = dot(recv_cols(base), ga[...])
        if live is not None:
            pulled = pulled * live
        egn = upstream_rows.astype(F32) + pulled
        egs = norm_back(normed[base : base + TILE, :], inverse[base : base + TILE, 0:1], egn)
        if live is not None:
            egs = egs * live
        egs = egs.astype(BF16)
        egf = (dot_nt(egs, w2[...]) * slope[base : base + TILE, :]).astype(BF16)
        g2[...] += dot_tn(active[base : base + TILE, :], egs)
        g1[0:width, :] += dot_tn(edges, egf)
        g1[width : 2 * width, :] += dot_tn(senders[base : base + TILE, :], egf)
        g_recv[...] += dot(recv_rows(base, False), egf)
        return egf, (egn + dot_nt(egf, w1[0:width, :])).astype(BF16)

    loads.up_long.wait()
    egf, grad = backward(long_tile, longs[...], up_long[...], live)
    refs.v_gl[...] = grad
    store(refs.v_gl, refs.out_gl)
    by_coarse = Sum(me, refs, "c")
    coarse_rows = COARSE_DEV * depth
    sources = idx[3:4, long_tile : long_tile + long_count]
    for patch in range(0, patches, 4):
        spots = lax.broadcasted_iota(jnp.int32, (4 * coarse_rows, long_count), 0)
        sums = dot(marks(spots + patch * coarse_rows == sources), egf)
        by_coarse.put_all(0, sums, 4, patch)
    by_coarse.start()
    by_node.first()

    loads.up_fine.wait()
    for step in range(fine_tiles):
        base = step * TILE
        egf, grad = backward(base, fine[base : base + TILE, :], up_fine[base : base + TILE, :], None)
        refs.v_gf[base : base + TILE, :] = grad
        spots = lax.broadcasted_iota(jnp.int32, (ext_rows, TILE), 0)
        g_ext[...] += dot(marks(spots == idx[0:1, base : base + TILE]), egf)
        if step == 0:
            by_coarse.first()
        if step == fine_tiles - 1:
            by_node.second()

    halo_out, back = refs.halo_out, refs.back
    halo_out[...] = g_ext[count:ext_rows, :].astype(BF16).reshape(depth + 2, hb, width)
    returns = []
    for by in range(1, depth):
        peer = me.along_z(by)
        sems = refs.rsub_sem.at[0, by - 1], refs.rsub_sem.at[1, by - 1]
        returns.append(send(halo_out.at[peer[1]], back.at[me.z], *sems, peer))
    for k, peer in enumerate((me.previous_patch(), me.next_patch())):
        sems = refs.rpat_sem.at[0, k], refs.rpat_sem.at[1, k]
        returns.append(send(halo_out.at[depth + k], back.at[depth + k], *sems, peer))
    back[me.z] = halo_out[me.z]

    high_part, low_part = split(g_recv[...])
    g1[2 * width : 3 * width, :] = dot_tn(node_rows, high_part) + dot_tn(node_rows, low_part)
    by_edge = Sum(me, refs, "e")
    by_edge.put_all(0, g1, patches)
    by_edge.put_all(per[0], g2, patches)
    by_edge.start()
    store(refs.v_gf, refs.out_gf)
    receiver_w = w1[2 * width : 3 * width, :]
    local[...] += dot_nt(high_part, receiver_w) + dot_nt(low_part, receiver_w)

    by_coarse.second()
    by_edge.first()
    by_node.across(row_blocks(by_node.patch_total()))
    sums = by_coarse.patch_total()
    by_coarse.across(
        [
            jnp.concatenate([part[8 * k : 8 * (k + 1), :] for part in sums], axis=0)
            for k in range(depth)
        ]
    )
    for copy in returns:
        copy.wait()
    picks = marks(lax.broadcasted_iota(jnp.int32, (count, lists.shape[1]), 0) == lists[...])
    sent = g_ext[0:count, :] + dot(picks, back[...].reshape((depth + 2) * hb, width))
    by_node.share(by_node.cross_total())
    by_edge.second()

    total = by_coarse.cross_total()[0]
    coarse = jnp.concatenate([total[0:8, :], total[8:16, :]], axis=1)
    sent = jnp.concatenate([sent[0:8, :] + coarse, sent[8:, :]], axis=0)
    high_part, low_part = split(sent)
    sender_w = w1[width : 2 * width, :]
    sent_grad = dot_nt(high_part, sender_w) + dot_nt(low_part, sender_w)
    refs.out_gn[...] = (local[...] + sent_grad).astype(BF16)

    by_edge.across(row_blocks(by_edge.patch_total()))
    by_edge.share(by_edge.cross_total())
    for group, outs in ((by_node, (refs.out_nw1, refs.out_nw2)), (by_edge, (refs.out_w1, refs.out_w2))):
        for copy in group.sharing:
            copy.wait_recv()
        at = 0
        for out in outs:
            for row in range(0, out.shape[0], 16):
                for part in (0, 1):
                    out[row : row + 16, part * columns : (part + 1) * columns] = group.block(at)
                    at += 1
    for group in (by_node, by_coarse, by_edge):
        group.wait_sends()
    for copy in halo:
        copy.wait_send()
    for copy in stores:
        copy.wait()


def whole(side, depth, arrays):
    shapes = SimpleNamespace(**{name: array.shape for name, array in arrays.items()})
    loaded = tuple(n for n in arrays if arrays[n].dtype == BF16 and n != "nodes")
    count, width = shapes.nodes
    half, columns = depth // 2, width // 2
    hb = shapes.sub_list[1]
    patches = 2 * side * side
    edges = shapes.fine[0] + shapes.longs[0]
    ext_rows = count + (depth + 2) * hb
    per = [dims[0] // patches for dims in (shapes.w1, shapes.w2, shapes.nw1, shapes.nw2)]
    sem = pltpu.SemaphoreType.DMA
    vmem = pl.BlockSpec(memory_space=pltpu.VMEM)
    any_space = pl.BlockSpec(memory_space=pl.ANY)

    outs = dict(
        out_node=(shapes.nodes, BF16),
        out_fine=(shapes.fine, BF16),
        out_long=(shapes.longs, BF16),
        out_gn=(shapes.nodes, BF16),
        out_gf=(shapes.fine, BF16),
        out_gl=(shapes.longs, BF16),
        out_w1=((per[0], width), F32),
        out_w2=((per[1], width), F32),
        out_nw1=((per[2], width), F32),
        out_nw2=((per[3], width), F32),
    )
    scratch = {"v_" + n: pltpu.VMEM(arrays[n].shape, BF16) for n in loaded}
    scratch |= dict(
        v_new_fine=pltpu.VMEM(shapes.fine, BF16),
        v_new_long=pltpu.VMEM(shapes.longs, BF16),
        v_gf=pltpu.VMEM(shapes.fine, BF16),
        v_gl=pltpu.VMEM(shapes.longs, BF16),
        load_sem=sem((len(loaded),)),
        store_sem=sem((4,)),
        ext=pltpu.VMEM((ext_rows, width), BF16),
        low=pltpu.VMEM((2, side, side, half, 16, columns), BF16),
        high=pltpu.VMEM((2, side, side, half, 16, columns), BF16),
        rows=pltpu.VMEM((depth + 2, hb, width), BF16),
        lists=pltpu.VMEM((1, (depth + 2) * hb), jnp.int32),
        idx=pltpu.VMEM((8, edges), jnp.int32),
        cols=pltpu.VMEM((edges, 8), jnp.int32),
        slope=pltpu.VMEM((edges, width), F32),
        active=pltpu.VMEM((edges, width), BF16),
        normed=pltpu.VMEM((edges, width), F32),
        inverse=pltpu.VMEM((edges, 128), F32),
        senders=pltpu.VMEM((edges, width), BF16),
        recv_proj=pltpu.VMEM((2 * count, width), BF16),
        agg=pltpu.VMEM((count, width), F32),
        ga=pltpu.VMEM((2 * count, width), BF16),
        g1=pltpu.VMEM(shapes.w1, F32),
        g2=pltpu.VMEM(shapes.w2, F32),
        g_recv=pltpu.VMEM((count, width), F32),
        g_ext=pltpu.VMEM((ext_rows, width), F32),
        local=pltpu.VMEM((count, width), F32),
        halo_out=pltpu.VMEM((depth + 2, hb, width), BF16),
        back=pltpu.VMEM((depth + 2, hb, width), BF16),
        zs_sem=sem((2, depth - 1)),
        sub_sem=sem((2, depth - 1)),
        pat_sem=sem((2, 2)),
        ab_sem=sem((2, 2, 2, side - 1)),
        cc_sem=sem((2, 2)),
        rsub_sem=sem((2, depth - 1)),
        rpat_sem=sem((2, 2)),
    )
    groups = dict(
        n=(per[2] + per[3], 2 * (per[2] + per[3]) // 16),
        c=(COARSE_DEV * depth, depth),
        e=(per[0] + per[1], 2 * (per[0] + per[1]) // 16),
    )
    for key, (rows, blocks) in groups.items():
        for field, kind in sum_scratch(side, depth, rows, columns, blocks).items():
            scratch[key + "_" + field] = kind
    names = (*arrays, *outs, *scratch)
    return pl.pallas_call(
        functools.partial(whole_kernel, side, depth, names, loaded),
        out_shape=tuple(jax.ShapeDtypeStruct(dims, kind) for dims, kind in outs.values()),
        in_specs=[any_space if n in loaded else vmem for n in arrays],
        out_specs=tuple(
            any_space if kind == BF16 and dims[0] > count else vmem for dims, kind in outs.values()
        ),
        scratch_shapes=list(scratch.values()),
        compiler_params=pltpu.CompilerParams(
            collective_id=0, has_side_effects=True, vmem_limit_bytes=VMEM_BYTES
        ),
        name="whole_layer",
    )(*arrays.values())


def hand_over_kernel(number, *refs):
    held, sems = refs[2 * number : 3 * number], refs[3 * number]
    arriving = [
        pltpu.make_async_copy(refs[k], held[k], sems.at[0, k]) for k in range(number)
    ]
    leaving = [
        pltpu.make_async_copy(held[k], refs[number + k], sems.at[1, k]) for k in range(number)
    ]
    for copy in arriving:
        copy.start()
    for k in range(number):
        arriving[k].wait()
        leaving[k].start()
    for copy in leaving:
        copy.wait()


def hand_over(results):
    number = len(results)
    any_space = pl.BlockSpec(memory_space=pl.ANY)
    return pl.pallas_call(
        functools.partial(hand_over_kernel, number),
        out_shape=tuple(jax.ShapeDtypeStruct(r.shape, r.dtype) for r in results),
        in_specs=[any_space] * number,
        out_specs=(any_space,) * number,
        scratch_shapes=[pltpu.VMEM(r.shape, r.dtype) for r in results]
        + [pltpu.SemaphoreType.DMA((2, number))],
        compiler_params=pltpu.CompilerParams(vmem_limit_bytes=VMEM_BYTES),
        name="hand_over",
    )(*results)


def per_device(
    side,
    depth,
    nodes,
    fine_edges,
    long_edges,
    fine_send,
    fine_recv,
    long_send,
    long_recv,
    long_mask,
    sub_list,
    patch_list,
    edge_w1,
    edge_w2,
    node_w1,
    node_w2,
    upstream_nodes,
    upstream_fine,
    upstream_long,
):
    def tiles(values):
        return values.reshape(-1, 128)

    arrays = dict(
        nodes=nodes,
        fine_send=tiles(fine_send),
        fine_recv=tiles(fine_recv),
        long_send=tiles(long_send),
        long_recv=tiles(long_recv),
        long_mask=tiles(long_mask),
        sub_list=sub_list,
        patch_list=patch_list,
        w1=edge_w1,
        fine=fine_edges,
        w2=edge_w2,
        longs=long_edges,
        nw1=node_w1,
        nw2=node_w2,
        up_nodes=upstream_nodes,
        up_long=upstream_long,
        up_fine=upstream_fine,
    )
    return hand_over(whole(side, depth, arrays))


def solution(mesh):
    side = math.isqrt(mesh.shape["patch"] // 2)
    depth = mesh.shape["sub"]
    rows = P(("patch", "sub"), None)
    flat = P(("patch", "sub"))
    return jax.shard_map(
        functools.partial(per_device, side, depth),
        mesh=mesh,
        in_specs=(rows,) * 3 + (flat,) * 5 + (rows,) * 2 + (P(),) * 4 + (rows,) * 3,
        out_specs=(rows,) * 6 + (P("patch", None),) * 4,
        check_vma=False,
    )
```

```python
import functools
import math
from types import SimpleNamespace

import jax
import jax.numpy as jnp
from jax import lax
from jax.experimental import pallas as pl
from jax.experimental.pallas import tpu as pltpu
from jax.sharding import PartitionSpec as P

COARSE_DEV = 8
F32 = jnp.float32
BF16 = jnp.bfloat16
MESH = pl.DeviceIdType.MESH
EPS = 1e-05
TILE = 256
VMEM_BYTES = 56 * 1024 * 1024


def dot(left, right):
    return jnp.dot(left, right, preferred_element_type=F32)


def dot_tn(left, right):
    return lax.dot_general(left, right, (((0,), (0,)), ((), ())), preferred_element_type=F32)


def dot_nt(left, right):
    return lax.dot_general(left, right, (((1,), (1,)), ((), ())), preferred_element_type=F32)


def split(values):
    high = values.astype(BF16)
    return high, (values - high.astype(F32)).astype(BF16)


def marks(hits):
    return jnp.where(hits, 1.0, 0.0).astype(BF16)


class Place:
    def __init__(self, side, depth):
        self.p = lax.axis_index("patch")
        self.z = lax.axis_index("sub")
        self.side, self.depth = side, depth
        self.core = lax.rem(self.p, 2)
        self.x = lax.rem(lax.div(self.p, 2), side)
        self.y = lax.div(self.p, 2 * side)
        self.patches = 2 * side * side

    def at(self, y, x, core):
        return (y * self.side + x) * 2 + core

    def along_x(self, by):
        return (self.at(self.y, lax.rem(self.x + by, self.side), self.core), self.z)

    def along_y(self, by):
        return (self.at(lax.rem(self.y + by, self.side), self.x, self.core), self.z)

    def along_z(self, by):
        return (self.p, lax.rem(self.z + by, self.depth))

    def other_core(self):
        return (self.at(self.y, self.x, 1 - self.core), self.z)

    def next_patch(self):
        return (lax.rem(self.p + 1, self.patches), self.z)

    def previous_patch(self):
        return (lax.rem(self.p + self.patches - 1, self.patches), self.z)

    def greet(self):
        peers = [self.along_x(by) for by in range(1, self.side)]
        peers += [self.along_y(by) for by in range(1, self.side)]
        peers += [self.along_z(by) for by in range(1, self.depth)]
        peers += [self.other_core(), self.next_patch(), self.previous_patch()]
        for peer in peers:
            pl.semaphore_signal(
                pltpu.get_barrier_semaphore(), inc=1, device_id=peer, device_id_type=MESH
            )
        return len(peers)


def far_first(peers):
    return sorted(range(1, peers), key=lambda by: -min(by, peers - by))


def remote(source, target, sent, landed, peer):
    return pltpu.make_async_remote_copy(
        src_ref=source,
        dst_ref=target,
        send_sem=sent,
        recv_sem=landed,
        device_id=peer,
        device_id_type=MESH,
    )


def send(source, target, sent, landed, peer):
    copy = remote(source, target, sent, landed, peer)
    copy.start()
    return copy


def norm_rows(values):
    centered = values - jnp.mean(values, axis=-1, keepdims=True)
    inverse = lax.rsqrt(jnp.mean(centered * centered, axis=-1, keepdims=True) + EPS)
    return centered * inverse, inverse


def norm_back(normed, inverse, upstream):
    mean_grad = jnp.mean(upstream, axis=-1, keepdims=True)
    mean_prod = jnp.mean(upstream * normed, axis=-1, keepdims=True)
    return (upstream - mean_grad - normed * mean_prod) * inverse


def silu_and_slope(values):
    sigma = 0.5 + 0.5 * jnp.tanh(0.5 * values)
    active = values * sigma
    return active, sigma + active * (1.0 - sigma)


def coarse_spot(side, depth, coarse):
    block, row = coarse // COARSE_DEV, coarse % COARSE_DEV
    patch, z = block // depth, block % depth
    core, x, y = patch % 2, patch // 2 % side, patch // (2 * side)
    half = depth // 2
    lower = z < half
    major, minor = jnp.where(lower, y, x), jnp.where(lower, x, y)
    place = ((core * side + major) * side + minor) * half + z % half
    return 16 * (place + jnp.where(lower, 0, 2 * side * side * half)) + row


class Sum:
    def __init__(self, me, refs, name):
        self.me, self.side = me, me.side
        for key, ref in vars(refs).items():
            if key.startswith(name + "_"):
                setattr(self, key[len(name) + 1 :], ref)
        self.majors, self.minors = (me.x, me.y), (me.y, me.x)

    def put(self, patch, start, values):
        side, half = self.side, self.table.shape[-1]
        core, x, y = patch % 2, patch // 2 % side, patch // (2 * side)
        values = values.astype(BF16)
        rows = pl.ds(start, values.shape[0])
        self.table[core, 0, x, y, rows, :] = values[:, :half]
        self.table[core, 1, y, x, rows, :] = values[:, half:]

    def put_all(self, start, values, patches, first=0):
        per = values.shape[0] // patches
        for k in range(patches):
            self.put(first + k, start, values[k * per : (k + 1) * per, :])

    def start(self):
        self.cores = {}
        for by in [*far_first(self.side), 0]:
            for part in (0, 1):
                major = lax.rem(self.majors[part] + by, self.side)
                source = self.table.at[1 - self.me.core, part, major]
                sems = self.core_sem.at[0, part, by], self.core_sem.at[1, part, by]
                copy = send(source, self.other.at[part, major], *sems, self.me.other_core())
                self.cores[part, by] = copy

    def first(self):
        me = self.me
        self.firsts = []
        for by in [*far_first(self.side), 0]:
            for part in (0, 1):
                major = lax.rem(self.majors[part] + by, self.side)
                self.cores[part, by].wait_recv()
                spot = (me.core, part, major)
                self.table[spot] = self.table[spot] + self.other[part, major]
                if by:
                    peer = me.along_x(by) if part == 0 else me.along_y(by)
                    target = self.first_in.at[part, by - 1]
                    sems = self.first_sem.at[0, part, by - 1], self.first_sem.at[1, part, by - 1]
                    self.firsts.append(send(self.table.at[spot], target, *sems, peer))

    def second(self):
        me, side = self.me, self.side
        self.seconds = []
        for copy in self.firsts:
            copy.wait_recv()
        for by in [*far_first(side), 0]:
            for part in (0, 1):
                minor = lax.rem(self.minors[part] + by, side)
                total = self.table[me.core, part, self.majors[part], minor].astype(F32)
                for k in range(side - 1):
                    total = total + self.first_in[part, k, minor].astype(F32)
                self.middle[part, minor] = total.astype(BF16)
                if by:
                    peer = me.along_y(by) if part == 0 else me.along_x(by)
                    source, target = self.middle.at[part, minor], self.second_in.at[part, by - 1]
                    sems = self.second_sem.at[0, part, by - 1], self.second_sem.at[1, part, by - 1]
                    self.seconds.append(send(source, target, *sems, peer))

    def patch_total(self):
        for copy in self.seconds:
            copy.wait_recv()
        sums = []
        for part in (0, 1):
            total = self.middle[part, self.minors[part]].astype(F32)
            for k in range(self.side - 1):
                total = total + self.second_in[part, k].astype(F32)
            sums.append(total)
        return sums

    def across(self, blocks):
        me, depth = self.me, self.me.depth
        per = self.z_out.shape[1]
        for k in range(depth * per):
            if k < len(blocks):
                self.z_out[k // per, k % per] = blocks[k].astype(BF16)
            else:
                self.z_out[k // per, k % per] = jnp.zeros(self.z_out.shape[2:], BF16)
        self.crossing = []
        for by in far_first(depth):
            peer = me.along_z(by)
            sems = self.z_sem.at[0, by - 1], self.z_sem.at[1, by - 1]
            self.crossing.append(send(self.z_out.at[peer[1]], self.z_in.at[by - 1], *sems, peer))

    def cross_total(self):
        for copy in self.crossing:
            copy.wait_recv()
        total = self.z_out[self.me.z].astype(F32)
        for k in range(self.me.depth - 1):
            total = total + self.z_in[k].astype(F32)
        return total

    def share(self, total):
        me = self.me
        self.shares[me.z] = total.astype(BF16)
        self.sharing = []
        for by in far_first(me.depth):
            mine = self.shares.at[me.z]
            sems = self.w_sem.at[0, by - 1], self.w_sem.at[1, by - 1]
            self.sharing.append(send(mine, mine, *sems, me.along_z(by)))

    def block(self, k):
        per = self.shares.shape[1]
        return self.shares[k // per, k % per].astype(F32)

    def wait_sends(self):
        for copy in [*self.cores.values()] + self.firsts + self.seconds + self.crossing + self.sharing:
            copy.wait_send()

    sharing = []


def sum_scratch(side, depth, rows, half, blocks):
    per = -(-blocks // depth)
    sem = pltpu.SemaphoreType.DMA
    return dict(
        table=pltpu.VMEM((2, 2, side, side, rows, half), BF16),
        other=pltpu.VMEM((2, side, side, rows, half), BF16),
        first_in=pltpu.VMEM((2, side - 1, side, rows, half), BF16),
        middle=pltpu.VMEM((2, side, rows, half), BF16),
        second_in=pltpu.VMEM((2, side - 1, rows, half), BF16),
        z_out=pltpu.VMEM((depth, per, 16, half), BF16),
        z_in=pltpu.VMEM((depth - 1, per, 16, half), BF16),
        shares=pltpu.VMEM((depth, per, 16, half), BF16),
        core_sem=sem((2, 2, side)),
        first_sem=sem((2, 2, side - 1)),
        second_sem=sem((2, 2, side - 1)),
        z_sem=sem((2, depth - 1)),
        w_sem=sem((2, depth - 1)),
    )


def row_blocks(sums):
    return [part[at : at + 16, :] for at in range(0, sums[0].shape[0], 16) for part in sums]


def whole_kernel(side, depth, names, loaded, *all_refs):
    refs = SimpleNamespace(**dict(zip(names, all_refs)))
    me = Place(side, depth)
    nodes, ext, low, high, rows = refs.v_nodes, refs.ext, refs.low, refs.high, refs.rows
    idx, cols, lists = refs.idx, refs.cols, refs.lists
    count, width = nodes.shape
    half = depth // 2
    columns = width // 2
    hb = refs.v_sub_list.shape[1]
    fine_count = refs.fine.shape[0]
    long_count = refs.longs.shape[0]
    ext_rows = ext.shape[0]
    patches = 2 * side * side
    fine_tiles = fine_count // TILE
    long_tile = fine_count

    greeted = me.greet()
    loads = SimpleNamespace()

    def load(names):
        for name in names:
            source, target = getattr(refs, name), getattr(refs, "v_" + name)
            sem = refs.load_sem.at[loaded.index(name)]
            copy = pltpu.make_async_copy(source, target, sem)
            copy.start()
            setattr(loads, name, copy)

    load(loaded[:8])
    w1, w2, nw1, nw2 = refs.v_w1, refs.v_w2, refs.v_nw1, refs.v_nw2
    fine, longs, up_fine, up_long = refs.v_fine, refs.v_longs, refs.v_up_fine, refs.v_up_long

    loads.nodes.wait()
    first = nodes[0:16, :].astype(F32)[0:8, :]
    block = jnp.concatenate([first[:, :columns], first[:, columns:]], axis=0).astype(BF16)
    in_low = me.z < half
    z_low = lax.rem(me.z, half)

    @pl.when(in_low)
    def _():
        low[me.core, me.y, me.x, z_low] = block

    @pl.when(jnp.logical_not(in_low))
    def _():
        high[me.core, me.x, me.y, z_low] = block

    pl.semaphore_wait(pltpu.get_barrier_semaphore(), greeted)
    for by in far_first(depth):
        sems = refs.zs_sem.at[0, by - 1], refs.zs_sem.at[1, by - 1]

        @pl.when(in_low)
        def _():
            mine = low.at[me.core, me.y, me.x, z_low]
            send(mine, mine, *sems, me.along_z(by))

        @pl.when(jnp.logical_not(in_low))
        def _():
            mine = high.at[me.core, me.x, me.y, z_low]
            send(mine, mine, *sems, me.along_z(by))

    load(loaded[8:11])
    loads.sub_list.wait()
    loads.patch_list.wait()
    for k in range(depth):
        lists[0:1, k * hb : (k + 1) * hb] = refs.v_sub_list[k : k + 1, :]
    for k in range(2):
        lists[0:1, (depth + k) * hb : (depth + k + 1) * hb] = refs.v_patch_list[k : k + 1, :]
    picks = marks(lax.broadcasted_iota(jnp.int32, (count, lists.shape[1]), 0) == lists[...])
    rows[...] = dot_tn(picks, nodes[...]).astype(BF16).reshape(depth + 2, hb, width)

    own_rows = pl.ds(pl.multiple_of(count + hb * me.z, hb), hb)

    idx[...] = jnp.zeros_like(idx)
    for copy in (loads.fine_send, loads.fine_recv, loads.long_send, loads.long_recv, loads.long_mask):
        copy.wait()
    spots = coarse_spot(side, depth, refs.v_long_send[...])
    for k in range(fine_count // 128):
        lanes = slice(128 * k, 128 * (k + 1))
        idx[0:1, lanes] = refs.v_fine_send[k : k + 1, :]
        idx[1:2, lanes] = refs.v_fine_recv[k : k + 1, :]
    for k in range(long_count // 128):
        lanes = slice(fine_count + 128 * k, fine_count + 128 * (k + 1))
        idx[0:1, lanes] = spots[k : k + 1, :]
        idx[1:2, lanes] = refs.v_long_recv[k : k + 1, :]
        idx[2:3, lanes] = refs.v_long_mask[k : k + 1, :]
        idx[3:4, lanes] = refs.v_long_send[k : k + 1, :]
    cols[...] = idx[...].T
    ext[0:count, :] = nodes[...]
    ext[own_rows, :] = rows[me.z]
    agg, ga, g1 = refs.agg, refs.ga, refs.g1
    g_ext, recv_proj = refs.g_ext, refs.recv_proj
    agg[...] = jnp.zeros_like(agg)

    mine = low.at[0, 0, 0, 0]
    for by in range(1, depth):
        sems = refs.zs_sem.at[0, by - 1], refs.zs_sem.at[1, by - 1]
        remote(mine, mine, *sems, me.along_z(by)).wait()

    def spread(step, low_part, high_part):
        copies = []
        for by in far_first(side):
            along = (me.along_x(by), me.along_y(by))
            for k, part in enumerate((low_part, high_part)):
                sems = refs.ab_sem.at[0, step, k, by - 1], refs.ab_sem.at[1, step, k, by - 1]
                copies.append(send(part, part, *sems, along[(step + k) % 2]))
        return copies

    spreading = spread(0, low.at[me.core, me.y, me.x], high.at[me.core, me.x, me.y])
    halo = []
    for by in far_first(depth):
        peer = me.along_z(by)
        sems = refs.sub_sem.at[0, by - 1], refs.sub_sem.at[1, by - 1]
        halo.append(send(rows.at[peer[1]], ext.at[own_rows, :], *sems, peer))
    for k, peer in enumerate((me.next_patch(), me.previous_patch())):
        target = ext.at[pl.ds(count + hb * (depth + k), hb), :]
        sems = refs.pat_sem.at[0, k], refs.pat_sem.at[1, k]
        halo.append(send(rows.at[depth + k], target, *sems, peer))

    loads.w1.wait()
    high_part, low_part = split(dot(nodes[...], w1[2 * width : 3 * width, :]))
    recv_proj[0:count, :] = high_part
    recv_proj[count : 2 * count, :] = low_part
    load(loaded[11:])

    slope, active, normed, inverse = refs.slope, refs.active, refs.normed, refs.inverse
    senders = refs.senders

    def recv_cols(base):
        lanes = lax.broadcasted_iota(jnp.int32, (TILE, 2 * count), 1)
        return marks(lax.rem(lanes, count) == cols[base : base + TILE, 1:2])

    def recv_rows(base, live):
        spots = lax.broadcasted_iota(jnp.int32, (count, TILE), 0)
        hits = spots == idx[1:2, base : base + TILE]
        if live:
            hits = jnp.logical_and(hits, idx[2:3, base : base + TILE] > 0)
        return marks(hits)

    def forward(base, edges, sender, rest, live):
        senders[base : base + TILE, :] = sender
        act, slopes = silu_and_slope(rest + dot(sender, w1[width : 2 * width, :]))
        act = act.astype(BF16)
        slope[base : base + TILE, :] = slopes
        active[base : base + TILE, :] = act
        unit, scale = norm_rows(dot(act, w2[...]))
        normed[base : base + TILE, :] = unit
        inverse[base : base + TILE, :] = jnp.broadcast_to(scale, (TILE, 128))
        if live is not None:
            unit = unit * live
        new = (edges.astype(F32) + unit).astype(BF16)
        agg[...] += dot(recv_rows(base, live is not None), new)
        return new

    def sender_free(base, edges):
        return dot(edges, w1[0:width, :]) + dot(recv_cols(base), recv_proj[...])

    def pass_on(low_row, high_row):
        copies = []
        for k, (part, row) in enumerate(((low, low_row), (high, high_row))):
            sems = refs.cc_sem.at[0, k, row], refs.cc_sem.at[1, k, row]
            source = part.at[me.core, row]
            copies.append(send(source, source, *sems, me.other_core()))
        return copies

    loads.fine.wait()
    loads.w2.wait()
    for copy in spreading:
        copy.wait()
    spreading = spread(1, low.at[me.core, me.y], high.at[me.core, me.x])
    passing = pass_on(me.y, me.x)
    for copy in halo:
        copy.wait_recv()
    for step in range(fine_tiles):
        base = step * TILE
        edges = fine[base : base + TILE, :]
        lanes = lax.broadcasted_iota(jnp.int32, (TILE, ext_rows), 1)
        picks = marks(lanes == cols[base : base + TILE, 0:1])
        sender = dot(picks, ext[...]).astype(BF16)
        refs.v_new_fine[base : base + TILE, :] = forward(
            base, edges, sender, sender_free(base, edges), None
        )
    loads.longs.wait()
    edges = longs[...]
    rest = sender_free(long_tile, edges)
    for k, by in enumerate(far_first(side)[::-1]):
        for copy in spreading[2 * (side - 2 - k) : 2 * (side - 1 - k)]:
            copy.wait()
        passing += pass_on(lax.rem(me.y + side - by, side), lax.rem(me.x + side - by, side))

    spot = cols[long_tile : long_tile + long_count, 0:1]
    spots = jnp.concatenate([spot, spot + 8], axis=0)
    core_rows = math.prod(low.shape[1:-1])
    lanes = lax.broadcasted_iota(jnp.int32, (2 * long_count, core_rows), 1)

    def coarse_rows_of(core):
        halves = jnp.zeros((2 * long_count, columns), F32)
        for k, part in enumerate((low, high)):
            here = spots - (2 * k + core) * core_rows
            halves += dot(marks(lanes == here), part[core].reshape(core_rows, columns))
        return halves

    halves = coarse_rows_of(me.core)
    for copy in passing:
        copy.wait()
    halves += coarse_rows_of(1 - me.core)
    sender = jnp.concatenate([halves[:long_count, :], halves[long_count:, :]], axis=1).astype(BF16)
    live = cols[long_tile : long_tile + long_count, 2:3].astype(F32)
    refs.v_new_long[...] = forward(long_tile, edges, sender, rest, live)

    stores = []

    def store(source, target):
        copy = pltpu.make_async_copy(source, target, refs.store_sem.at[len(stores)])
        copy.start()
        stores.append(copy)


    loads.nw1.wait()
    loads.nw2.wait()
    loads.up_nodes.wait()
    node_rows = nodes[...]
    aggregate = agg[...].astype(BF16)
    node_first = dot(node_rows, nw1[0:width, :]) + dot(aggregate, nw1[width : 2 * width, :])
    node_active, node_slope = silu_and_slope(node_first)
    node_active = node_active.astype(BF16)
    node_normed, node_inverse = norm_rows(dot(node_active, nw2[...]))
    refs.out_node[...] = (node_rows.astype(F32) + node_normed).astype(BF16)
    upstream = refs.v_up_nodes[...].astype(F32)
    ngs = norm_back(node_normed, node_inverse, upstream).astype(BF16)
    ngf = (dot_nt(ngs, nw2[...]) * node_slope).astype(BF16)
    by_node = Sum(me, refs, "n")
    per = [ref.shape[0] // patches for ref in (w1, w2, nw1, nw2)]
    by_node.put_all(per[2], dot_tn(node_active, ngs), patches)
    by_node.put_all(0, dot_tn(node_rows, ngf), patches // 2)
    by_node.put_all(0, dot_tn(aggregate, ngf), patches // 2, patches // 2)
    by_node.start()
    local = refs.local
    local[...] = upstream + dot_nt(ngf, nw1[0:width, :])
    high_part, low_part = split(dot_nt(ngf, nw1[width : 2 * width, :]))
    ga[0:count, :] = high_part
    ga[count : 2 * count, :] = low_part

    egs_all, egf_all = refs.egs, refs.egf

    def backward(base, upstream_rows, live):
        pulled = dot(recv_cols(base), ga[...])
        if live is not None:
            pulled = pulled * live
        egn = upstream_rows.astype(F32) + pulled
        egs = norm_back(normed[base : base + TILE, :], inverse[base : base + TILE, 0:1], egn)
        normed[base : base + TILE, :] = egn
        if live is not None:
            egs = egs * live
        egs = egs.astype(BF16)
        egf = (dot_nt(egs, w2[...]) * slope[base : base + TILE, :]).astype(BF16)
        egs_all[base : base + TILE, :] = egs
        egf_all[base : base + TILE, :] = egf
        return egf

    def edge_grad(base):
        egf = egf_all[base : base + TILE, :]
        return (normed[base : base + TILE, :] + dot_nt(egf, w1[0:width, :])).astype(BF16)

    loads.up_long.wait()
    egf = backward(long_tile, up_long[...], live)
    by_coarse = Sum(me, refs, "c")
    coarse_rows = COARSE_DEV * depth
    sources = idx[3:4, long_tile : long_tile + long_count]
    for patch in range(0, patches, 4):
        spots = lax.broadcasted_iota(jnp.int32, (4 * coarse_rows, long_count), 0)
        sums = dot(marks(spots + patch * coarse_rows == sources), egf)
        by_coarse.put_all(0, sums, 4, patch)
    by_coarse.start()
    by_node.first()

    loads.up_fine.wait()
    for step in range(fine_tiles):
        base = step * TILE
        backward(base, up_fine[base : base + TILE, :], None)
    by_coarse.first()

    by_edge = Sum(me, refs, "e")
    by_edge.put_all(per[0], dot_tn(active[...], egs_all[...]), patches)
    fine_egf, long_egf = egf_all[0:fine_count, :], egf_all[fine_count:, :]
    spots = lax.broadcasted_iota(jnp.int32, (count, fine_count + long_count), 0)
    high_part, low_part = split(dot(marks(spots == idx[1:2, :]), egf_all[...]))
    g1[0:width, :] = dot_tn(fine[...], fine_egf) + dot_tn(longs[...], long_egf)
    g1[width : 2 * width, :] = dot_tn(senders[...], egf_all[...])
    g1[2 * width : 3 * width, :] = dot_tn(node_rows, high_part) + dot_tn(node_rows, low_part)
    by_edge.put_all(0, g1, patches)
    by_edge.start()

    spots = lax.broadcasted_iota(jnp.int32, (ext_rows, fine_count), 0)
    g_ext[...] = dot(marks(spots == idx[0:1, 0:fine_count]), fine_egf)
    halo_out, back = refs.halo_out, refs.back
    halo_out[...] = g_ext[count:ext_rows, :].astype(BF16).reshape(depth + 2, hb, width)
    returns = []
    for by in far_first(depth):
        peer = me.along_z(by)
        sems = refs.rsub_sem.at[0, by - 1], refs.rsub_sem.at[1, by - 1]
        returns.append(send(halo_out.at[peer[1]], back.at[me.z], *sems, peer))
    for k, peer in enumerate((me.previous_patch(), me.next_patch())):
        sems = refs.rpat_sem.at[0, k], refs.rpat_sem.at[1, k]
        returns.append(send(halo_out.at[depth + k], back.at[depth + k], *sems, peer))
    back[me.z] = halo_out[me.z]

    by_node.second()
    receiver_w = w1[2 * width : 3 * width, :]
    local[...] += dot_nt(high_part, receiver_w) + dot_nt(low_part, receiver_w)
    by_edge.first()
    store(refs.v_new_fine, refs.out_fine)
    store(refs.v_new_long, refs.out_long)
    for step in range(fine_tiles - 1):
        base = step * TILE
        refs.v_gf[base : base + TILE, :] = edge_grad(base)
    by_node.across(row_blocks(by_node.patch_total()))
    by_coarse.second()
    base = fine_count - TILE
    refs.v_gf[base : base + TILE, :] = edge_grad(base)
    refs.v_gl[...] = edge_grad(long_tile)
    store(refs.v_gf, refs.out_gf)
    store(refs.v_gl, refs.out_gl)
    by_edge.second()
    by_node.share(by_node.cross_total())
    sums = by_coarse.patch_total()
    by_coarse.across(
        [
            jnp.concatenate([part[8 * k : 8 * (k + 1), :] for part in sums], axis=0)
            for k in range(depth)
        ]
    )
    for copy in returns:
        copy.wait()
    picks = marks(lax.broadcasted_iota(jnp.int32, (count, lists.shape[1]), 0) == lists[...])
    sent = g_ext[0:count, :] + dot(picks, back[...].reshape((depth + 2) * hb, width))
    by_edge.across(row_blocks(by_edge.patch_total()))

    total = by_coarse.cross_total()[0]
    coarse = jnp.concatenate([total[0:8, :], total[8:16, :]], axis=1)
    sent = jnp.concatenate([sent[0:8, :] + coarse, sent[8:, :]], axis=0)
    high_part, low_part = split(sent)
    sender_w = w1[width : 2 * width, :]
    sent_grad = dot_nt(high_part, sender_w) + dot_nt(low_part, sender_w)
    refs.out_gn[...] = (local[...] + sent_grad).astype(BF16)

    by_edge.share(by_edge.cross_total())
    for group, outs in ((by_node, (refs.out_nw1, refs.out_nw2)), (by_edge, (refs.out_w1, refs.out_w2))):
        for copy in group.sharing:
            copy.wait_recv()
        at = 0
        for out in outs:
            for row in range(0, out.shape[0], 16):
                for part in (0, 1):
                    out[row : row + 16, part * columns : (part + 1) * columns] = group.block(at)
                    at += 1
    for group in (by_node, by_coarse, by_edge):
        group.wait_sends()
    for copy in halo:
        copy.wait_send()
    for copy in stores:
        copy.wait()


def whole(side, depth, arrays):
    shapes = SimpleNamespace(**{name: array.shape for name, array in arrays.items()})
    loaded = tuple(arrays)
    count, width = shapes.nodes
    half, columns = depth // 2, width // 2
    hb = shapes.sub_list[1]
    patches = 2 * side * side
    edges = shapes.fine[0] + shapes.longs[0]
    ext_rows = count + (depth + 2) * hb
    per = [dims[0] // patches for dims in (shapes.w1, shapes.w2, shapes.nw1, shapes.nw2)]
    sem = pltpu.SemaphoreType.DMA
    vmem = pl.BlockSpec(memory_space=pltpu.VMEM)
    any_space = pl.BlockSpec(memory_space=pl.ANY)

    outs = dict(
        out_node=(shapes.nodes, BF16),
        out_fine=(shapes.fine, BF16),
        out_long=(shapes.longs, BF16),
        out_gn=(shapes.nodes, BF16),
        out_gf=(shapes.fine, BF16),
        out_gl=(shapes.longs, BF16),
        out_w1=((per[0], width), F32),
        out_w2=((per[1], width), F32),
        out_nw1=((per[2], width), F32),
        out_nw2=((per[3], width), F32),
    )
    scratch = {"v_" + n: pltpu.VMEM(arrays[n].shape, arrays[n].dtype) for n in loaded}
    scratch |= dict(
        v_new_fine=pltpu.VMEM(shapes.fine, BF16),
        v_new_long=pltpu.VMEM(shapes.longs, BF16),
        v_gf=pltpu.VMEM(shapes.fine, BF16),
        v_gl=pltpu.VMEM(shapes.longs, BF16),
        load_sem=sem((len(loaded),)),
        store_sem=sem((4,)),
        ext=pltpu.VMEM((ext_rows, width), BF16),
        low=pltpu.VMEM((2, side, side, half, 16, columns), BF16),
        high=pltpu.VMEM((2, side, side, half, 16, columns), BF16),
        rows=pltpu.VMEM((depth + 2, hb, width), BF16),
        lists=pltpu.VMEM((1, (depth + 2) * hb), jnp.int32),
        idx=pltpu.VMEM((8, edges), jnp.int32),
        cols=pltpu.VMEM((edges, 8), jnp.int32),
        slope=pltpu.VMEM((edges, width), F32),
        active=pltpu.VMEM((edges, width), BF16),
        normed=pltpu.VMEM((edges, width), F32),
        inverse=pltpu.VMEM((edges, 128), F32),
        senders=pltpu.VMEM((edges, width), BF16),
        recv_proj=pltpu.VMEM((2 * count, width), BF16),
        agg=pltpu.VMEM((count, width), F32),
        ga=pltpu.VMEM((2 * count, width), BF16),
        g1=pltpu.VMEM(shapes.w1, F32),
        egs=pltpu.VMEM((edges, width), BF16),
        egf=pltpu.VMEM((edges, width), BF16),
        g_ext=pltpu.VMEM((ext_rows, width), F32),
        local=pltpu.VMEM((count, width), F32),
        halo_out=pltpu.VMEM((depth + 2, hb, width), BF16),
        back=pltpu.VMEM((depth + 2, hb, width), BF16),
        zs_sem=sem((2, depth - 1)),
        sub_sem=sem((2, depth - 1)),
        pat_sem=sem((2, 2)),
        ab_sem=sem((2, 2, 2, side - 1)),
        cc_sem=sem((2, 2, side)),
        rsub_sem=sem((2, depth - 1)),
        rpat_sem=sem((2, 2)),
    )
    groups = dict(
        n=(per[2] + per[3], 2 * (per[2] + per[3]) // 16),
        c=(COARSE_DEV * depth, depth),
        e=(per[0] + per[1], 2 * (per[0] + per[1]) // 16),
    )
    for key, (rows, blocks) in groups.items():
        for field, kind in sum_scratch(side, depth, rows, columns, blocks).items():
            scratch[key + "_" + field] = kind
    names = (*arrays, *outs, *scratch)
    return pl.pallas_call(
        functools.partial(whole_kernel, side, depth, names, loaded),
        out_shape=tuple(jax.ShapeDtypeStruct(dims, kind) for dims, kind in outs.values()),
        in_specs=[any_space] * len(arrays),
        out_specs=tuple(
            any_space if kind == BF16 and dims[0] > count else vmem for dims, kind in outs.values()
        ),
        scratch_shapes=list(scratch.values()),
        compiler_params=pltpu.CompilerParams(
            collective_id=0, has_side_effects=True, vmem_limit_bytes=VMEM_BYTES
        ),
        name="whole_layer",
    )(*arrays.values())


def hand_over_kernel(number, *refs):
    held, sems = refs[2 * number : 3 * number], refs[3 * number]
    arriving = [
        pltpu.make_async_copy(refs[k], held[k], sems.at[0, k]) for k in range(number)
    ]
    leaving = [
        pltpu.make_async_copy(held[k], refs[number + k], sems.at[1, k]) for k in range(number)
    ]
    for copy in arriving:
        copy.start()
    for k in range(number):
        arriving[k].wait()
        leaving[k].start()
    for copy in leaving:
        copy.wait()


def hand_over(results):
    number = len(results)
    any_space = pl.BlockSpec(memory_space=pl.ANY)
    return pl.pallas_call(
        functools.partial(hand_over_kernel, number),
        out_shape=tuple(jax.ShapeDtypeStruct(r.shape, r.dtype) for r in results),
        in_specs=[any_space] * number,
        out_specs=(any_space,) * number,
        scratch_shapes=[pltpu.VMEM(r.shape, r.dtype) for r in results]
        + [pltpu.SemaphoreType.DMA((2, number))],
        compiler_params=pltpu.CompilerParams(vmem_limit_bytes=VMEM_BYTES),
        name="hand_over",
    )(*results)


def per_device(
    side,
    depth,
    nodes,
    fine_edges,
    long_edges,
    fine_send,
    fine_recv,
    long_send,
    long_recv,
    long_mask,
    sub_list,
    patch_list,
    edge_w1,
    edge_w2,
    node_w1,
    node_w2,
    upstream_nodes,
    upstream_fine,
    upstream_long,
):
    def tiles(values):
        return values.reshape(-1, 128)

    arrays = dict(
        nodes=nodes,
        fine_send=tiles(fine_send),
        fine_recv=tiles(fine_recv),
        long_send=tiles(long_send),
        long_recv=tiles(long_recv),
        long_mask=tiles(long_mask),
        sub_list=sub_list,
        patch_list=patch_list,
        w1=edge_w1,
        fine=fine_edges,
        w2=edge_w2,
        longs=long_edges,
        nw1=node_w1,
        nw2=node_w2,
        up_nodes=upstream_nodes,
        up_long=upstream_long,
        up_fine=upstream_fine,
    )
    return hand_over(whole(side, depth, arrays))


def solution(mesh):
    side = math.isqrt(mesh.shape["patch"] // 2)
    depth = mesh.shape["sub"]
    rows = P(("patch", "sub"), None)
    flat = P(("patch", "sub"))
    return jax.shard_map(
        functools.partial(per_device, side, depth),
        mesh=mesh,
        in_specs=(rows,) * 3 + (flat,) * 5 + (rows,) * 2 + (P(),) * 4 + (rows,) * 3,
        out_specs=(rows,) * 6 + (P("patch", None),) * 4,
        check_vma=False,
    )
```

```python
import functools
import math
from types import SimpleNamespace

import jax
import jax.numpy as jnp
from jax import lax
from jax.experimental import pallas as pl
from jax.experimental.pallas import tpu as pltpu
from jax.sharding import PartitionSpec as P

COARSE_DEV = 8
F32 = jnp.float32
BF16 = jnp.bfloat16
MESH = pl.DeviceIdType.MESH
EPS = 1e-05
TILE = 256
VMEM_BYTES = 56 * 1024 * 1024


def dot(left, right):
    return jnp.dot(left, right, preferred_element_type=F32)


def dot_tn(left, right):
    return lax.dot_general(left, right, (((0,), (0,)), ((), ())), preferred_element_type=F32)


def dot_nt(left, right):
    return lax.dot_general(left, right, (((1,), (1,)), ((), ())), preferred_element_type=F32)


def split(values):
    high = values.astype(BF16)
    return high, (values - high.astype(F32)).astype(BF16)


def marks(hits):
    return jnp.where(hits, 1.0, 0.0).astype(BF16)


class Place:
    def __init__(self, side, depth):
        self.p = lax.axis_index("patch")
        self.z = lax.axis_index("sub")
        self.side, self.depth = side, depth
        self.core = lax.rem(self.p, 2)
        self.x = lax.rem(lax.div(self.p, 2), side)
        self.y = lax.div(self.p, 2 * side)
        self.patches = 2 * side * side

    def at(self, y, x, core):
        return (y * self.side + x) * 2 + core

    def along_x(self, by):
        return (self.at(self.y, lax.rem(self.x + by, self.side), self.core), self.z)

    def along_y(self, by):
        return (self.at(lax.rem(self.y + by, self.side), self.x, self.core), self.z)

    def along_z(self, by):
        return (self.p, lax.rem(self.z + by, self.depth))

    def other_core(self):
        return (self.at(self.y, self.x, 1 - self.core), self.z)

    def next_patch(self):
        return (lax.rem(self.p + 1, self.patches), self.z)

    def previous_patch(self):
        return (lax.rem(self.p + self.patches - 1, self.patches), self.z)

    def greet(self):
        peers = [self.along_z(by) for by in far_first(self.depth)]
        peers += [self.along_x(by) for by in far_first(self.side)]
        peers += [self.along_y(by) for by in far_first(self.side)]
        peers += [self.other_core(), self.next_patch(), self.previous_patch()]
        for peer in peers:
            pl.semaphore_signal(
                pltpu.get_barrier_semaphore(), inc=1, device_id=peer, device_id_type=MESH
            )
        return len(peers)


def far_first(peers):
    return sorted(range(1, peers), key=lambda by: -min(by, peers - by))


def remote(source, target, sent, landed, peer):
    return pltpu.make_async_remote_copy(
        src_ref=source,
        dst_ref=target,
        send_sem=sent,
        recv_sem=landed,
        device_id=peer,
        device_id_type=MESH,
    )


def send(source, target, sent, landed, peer):
    copy = remote(source, target, sent, landed, peer)
    copy.start()
    return copy


def norm_rows(values):
    centered = values - jnp.mean(values, axis=-1, keepdims=True)
    inverse = lax.rsqrt(jnp.mean(centered * centered, axis=-1, keepdims=True) + EPS)
    return centered * inverse, inverse


def norm_back(normed, inverse, upstream):
    mean_grad = jnp.mean(upstream, axis=-1, keepdims=True)
    mean_prod = jnp.mean(upstream * normed, axis=-1, keepdims=True)
    return (upstream - mean_grad - normed * mean_prod) * inverse


def silu_and_slope(values):
    sigma = 0.5 + 0.5 * jnp.tanh(0.5 * values)
    active = values * sigma
    return active, sigma + active * (1.0 - sigma)


def coarse_spot(side, depth, coarse):
    block, row = coarse // COARSE_DEV, coarse % COARSE_DEV
    patch, z = block // depth, block % depth
    core, x, y = patch % 2, patch // 2 % side, patch // (2 * side)
    half = depth // 2
    lower = z < half
    major, minor = jnp.where(lower, y, x), jnp.where(lower, x, y)
    place = ((core * side + major) * side + minor) * half + z % half
    return 16 * (place + jnp.where(lower, 0, 2 * side * side * half)) + row


class Sum:
    def __init__(self, me, refs, name):
        self.me, self.side = me, me.side
        for key, ref in vars(refs).items():
            if key.startswith(name + "_"):
                setattr(self, key[len(name) + 1 :], ref)
        self.majors, self.minors = (me.x, me.y), (me.y, me.x)

    def put(self, patch, start, values):
        side, half = self.side, self.table.shape[-1]
        core, x, y = patch % 2, patch // 2 % side, patch // (2 * side)
        values = values.astype(BF16)
        rows = pl.ds(start, values.shape[0])
        self.table[core, 0, x, y, rows, :] = values[:, :half]
        self.table[core, 1, y, x, rows, :] = values[:, half:]

    def put_all(self, start, values, patches, first=0):
        per = values.shape[0] // patches
        for k in range(patches):
            self.put(first + k, start, values[k * per : (k + 1) * per, :])

    def start(self, in_pieces=False):
        self.cores = {}
        for by in [*far_first(self.side), 0] if in_pieces else [None]:
            for part in (0, 1):
                source, target = self.table.at[1 - self.me.core, part], self.other.at[part]
                if in_pieces:
                    major = lax.rem(self.majors[part] + by, self.side)
                    source, target = source.at[major], target.at[major]
                sems = self.core_sem.at[0, part, by or 0], self.core_sem.at[1, part, by or 0]
                self.cores[part, by] = send(source, target, *sems, self.me.other_core())

    def first(self):
        me = self.me
        self.firsts = []
        for part in (0, 1):
            if (part, None) in self.cores:
                self.cores[part, None].wait_recv()
        for by in [*far_first(self.side), 0]:
            for part in (0, 1):
                major = lax.rem(self.majors[part] + by, self.side)
                if (part, by) in self.cores:
                    self.cores[part, by].wait_recv()
                spot = (me.core, part, major)
                self.table[spot] = self.table[spot] + self.other[part, major]
                if by:
                    peer = me.along_x(by) if part == 0 else me.along_y(by)
                    target = self.first_in.at[part, by - 1]
                    sems = self.first_sem.at[0, part, by - 1], self.first_sem.at[1, part, by - 1]
                    self.firsts.append(send(self.table.at[spot], target, *sems, peer))

    def second(self):
        me, side = self.me, self.side
        self.seconds = []
        for copy in self.firsts:
            copy.wait_recv()
        for by in [*far_first(side), 0]:
            for part in (0, 1):
                minor = lax.rem(self.minors[part] + by, side)
                total = self.table[me.core, part, self.majors[part], minor].astype(F32)
                for k in range(side - 1):
                    total = total + self.first_in[part, k, minor].astype(F32)
                self.middle[part, minor] = total.astype(BF16)
                if by:
                    peer = me.along_y(by) if part == 0 else me.along_x(by)
                    source, target = self.middle.at[part, minor], self.second_in.at[part, by - 1]
                    sems = self.second_sem.at[0, part, by - 1], self.second_sem.at[1, part, by - 1]
                    self.seconds.append(send(source, target, *sems, peer))

    def patch_total(self):
        for copy in self.seconds:
            copy.wait_recv()
        sums = []
        for part in (0, 1):
            total = self.middle[part, self.minors[part]].astype(F32)
            for k in range(self.side - 1):
                total = total + self.second_in[part, k].astype(F32)
            sums.append(total)
        return sums

    def across(self, blocks):
        me, depth = self.me, self.me.depth
        per = self.z_out.shape[1]
        for k in range(depth * per):
            if k < len(blocks):
                self.z_out[k // per, k % per] = blocks[k].astype(BF16)
            else:
                self.z_out[k // per, k % per] = jnp.zeros(self.z_out.shape[2:], BF16)
        self.crossing = []
        for by in far_first(depth):
            peer = me.along_z(by)
            sems = self.z_sem.at[0, by - 1], self.z_sem.at[1, by - 1]
            self.crossing.append(send(self.z_out.at[peer[1]], self.z_in.at[by - 1], *sems, peer))

    def cross_total(self):
        for copy in self.crossing:
            copy.wait_recv()
        total = self.z_out[self.me.z].astype(F32)
        for k in range(self.me.depth - 1):
            total = total + self.z_in[k].astype(F32)
        return total

    def share(self, total):
        me = self.me
        self.shares[me.z] = total.astype(BF16)
        self.sharing = []
        for by in far_first(me.depth):
            mine = self.shares.at[me.z]
            sems = self.w_sem.at[0, by - 1], self.w_sem.at[1, by - 1]
            self.sharing.append(send(mine, mine, *sems, me.along_z(by)))

    def block(self, k):
        per = self.shares.shape[1]
        return self.shares[k // per, k % per].astype(F32)

    def wait_sends(self):
        for copy in [*self.cores.values()] + self.firsts + self.seconds + self.crossing + self.sharing:
            copy.wait_send()

    sharing = []


def sum_scratch(side, depth, rows, half, blocks):
    per = -(-blocks // depth)
    sem = pltpu.SemaphoreType.DMA
    return dict(
        table=pltpu.VMEM((2, 2, side, side, rows, half), BF16),
        other=pltpu.VMEM((2, side, side, rows, half), BF16),
        first_in=pltpu.VMEM((2, side - 1, side, rows, half), BF16),
        middle=pltpu.VMEM((2, side, rows, half), BF16),
        second_in=pltpu.VMEM((2, side - 1, rows, half), BF16),
        z_out=pltpu.VMEM((depth, per, 16, half), BF16),
        z_in=pltpu.VMEM((depth - 1, per, 16, half), BF16),
        shares=pltpu.VMEM((depth, per, 16, half), BF16),
        core_sem=sem((2, 2, side)),
        first_sem=sem((2, 2, side - 1)),
        second_sem=sem((2, 2, side - 1)),
        z_sem=sem((2, depth - 1)),
        w_sem=sem((2, depth - 1)),
    )


def row_blocks(sums):
    return [part[at : at + 16, :] for at in range(0, sums[0].shape[0], 16) for part in sums]


def whole_kernel(side, depth, names, loaded, *all_refs):
    refs = SimpleNamespace(**dict(zip(names, all_refs)))
    me = Place(side, depth)
    nodes, ext, low, high, rows = refs.v_nodes, refs.ext, refs.low, refs.high, refs.rows
    idx, cols, lists = refs.idx, refs.cols, refs.lists
    count, width = nodes.shape
    half = depth // 2
    columns = width // 2
    hb = refs.v_sub_list.shape[1]
    fine_count = refs.fine.shape[0]
    long_count = refs.longs.shape[0]
    ext_rows = ext.shape[0]
    patches = 2 * side * side
    fine_tiles = fine_count // TILE
    long_tile = fine_count

    loads = SimpleNamespace()

    def load(names):
        for name in names:
            source, target = getattr(refs, name), getattr(refs, "v_" + name)
            sem = refs.load_sem.at[loaded.index(name)]
            copy = pltpu.make_async_copy(source, target, sem)
            copy.start()
            setattr(loads, name, copy)

    load(loaded[:1])
    greeted = me.greet()
    w1, w2, nw1, nw2 = refs.v_w1, refs.v_w2, refs.v_nw1, refs.v_nw2
    fine, longs, up_fine, up_long = refs.v_fine, refs.v_longs, refs.v_up_fine, refs.v_up_long

    loads.nodes.wait()
    first = nodes[0:16, :].astype(F32)[0:8, :]
    block = jnp.concatenate([first[:, :columns], first[:, columns:]], axis=0).astype(BF16)
    in_low = me.z < half
    z_low = lax.rem(me.z, half)

    @pl.when(in_low)
    def _():
        low[me.core, me.y, me.x, z_low] = block

    @pl.when(jnp.logical_not(in_low))
    def _():
        high[me.core, me.x, me.y, z_low] = block

    pl.semaphore_wait(pltpu.get_barrier_semaphore(), greeted)
    for by in far_first(depth):
        sems = refs.zs_sem.at[0, by - 1], refs.zs_sem.at[1, by - 1]

        @pl.when(in_low)
        def _():
            mine = low.at[me.core, me.y, me.x, z_low]
            send(mine, mine, *sems, me.along_z(by))

        @pl.when(jnp.logical_not(in_low))
        def _():
            mine = high.at[me.core, me.x, me.y, z_low]
            send(mine, mine, *sems, me.along_z(by))

    load(loaded[1:11])
    loads.sub_list.wait()
    loads.patch_list.wait()
    for k in range(depth):
        lists[0:1, k * hb : (k + 1) * hb] = refs.v_sub_list[k : k + 1, :]
    for k in range(2):
        lists[0:1, (depth + k) * hb : (depth + k + 1) * hb] = refs.v_patch_list[k : k + 1, :]
    picks = marks(lax.broadcasted_iota(jnp.int32, (count, lists.shape[1]), 0) == lists[...])
    rows[...] = dot_tn(picks, nodes[...]).astype(BF16).reshape(depth + 2, hb, width)

    own_rows = pl.ds(pl.multiple_of(count + hb * me.z, hb), hb)

    idx[...] = jnp.zeros_like(idx)
    for copy in (loads.fine_send, loads.fine_recv, loads.long_send, loads.long_recv, loads.long_mask):
        copy.wait()
    spots = coarse_spot(side, depth, refs.v_long_send[...])
    for k in range(fine_count // 128):
        lanes = slice(128 * k, 128 * (k + 1))
        idx[0:1, lanes] = refs.v_fine_send[k : k + 1, :]
        idx[1:2, lanes] = refs.v_fine_recv[k : k + 1, :]
    for k in range(long_count // 128):
        lanes = slice(fine_count + 128 * k, fine_count + 128 * (k + 1))
        idx[0:1, lanes] = spots[k : k + 1, :]
        idx[1:2, lanes] = refs.v_long_recv[k : k + 1, :]
        idx[2:3, lanes] = refs.v_long_mask[k : k + 1, :]
        idx[3:4, lanes] = refs.v_long_send[k : k + 1, :]
    cols[...] = idx[...].T
    ext[0:count, :] = nodes[...]
    ext[own_rows, :] = rows[me.z]
    agg, ga = refs.agg, refs.ga
    g_ext, recv_proj = refs.g_ext, refs.recv_proj
    agg[...] = jnp.zeros_like(agg)

    mine = low.at[0, 0, 0, 0]
    for by in range(1, depth):
        sems = refs.zs_sem.at[0, by - 1], refs.zs_sem.at[1, by - 1]
        remote(mine, mine, *sems, me.along_z(by)).wait()

    def spread(step, low_part, high_part):
        copies = []
        for by in far_first(side):
            along = (me.along_x(by), me.along_y(by))
            for k, part in enumerate((low_part, high_part)):
                sems = refs.ab_sem.at[0, step, k, by - 1], refs.ab_sem.at[1, step, k, by - 1]
                copies.append(send(part, part, *sems, along[(step + k) % 2]))
        return copies

    spreading = spread(0, low.at[me.core, me.y, me.x], high.at[me.core, me.x, me.y])
    halo = []
    for by in far_first(depth):
        peer = me.along_z(by)
        sems = refs.sub_sem.at[0, by - 1], refs.sub_sem.at[1, by - 1]
        halo.append(send(rows.at[peer[1]], ext.at[own_rows, :], *sems, peer))
    for k, peer in enumerate((me.next_patch(), me.previous_patch())):
        target = ext.at[pl.ds(count + hb * (depth + k), hb), :]
        sems = refs.pat_sem.at[0, k], refs.pat_sem.at[1, k]
        halo.append(send(rows.at[depth + k], target, *sems, peer))

    loads.w1.wait()
    high_part, low_part = split(dot(nodes[...], w1[2 * width : 3 * width, :]))
    recv_proj[0:count, :] = high_part
    recv_proj[count : 2 * count, :] = low_part
    load(loaded[11:])

    slope, active, normed, inverse = refs.slope, refs.active, refs.normed, refs.inverse
    senders = refs.senders

    def recv_cols(base):
        lanes = lax.broadcasted_iota(jnp.int32, (TILE, 2 * count), 1)
        return marks(lax.rem(lanes, count) == cols[base : base + TILE, 1:2])

    def recv_rows(base, live):
        spots = lax.broadcasted_iota(jnp.int32, (count, TILE), 0)
        hits = spots == idx[1:2, base : base + TILE]
        if live:
            hits = jnp.logical_and(hits, idx[2:3, base : base + TILE] > 0)
        return marks(hits)

    def forward(base, edges, sender, rest, live):
        senders[base : base + TILE, :] = sender
        act, slopes = silu_and_slope(rest + dot(sender, w1[width : 2 * width, :]))
        act = act.astype(BF16)
        slope[base : base + TILE, :] = slopes
        active[base : base + TILE, :] = act
        unit, scale = norm_rows(dot(act, w2[...]))
        normed[base : base + TILE, :] = unit
        inverse[base : base + TILE, :] = jnp.broadcast_to(scale, (TILE, 128))
        if live is not None:
            unit = unit * live
        new = (edges.astype(F32) + unit).astype(BF16)
        agg[...] += dot(recv_rows(base, live is not None), new)
        return new

    def sender_free(base, edges):
        return dot(edges, w1[0:width, :]) + dot(recv_cols(base), recv_proj[...])

    def pass_on(low_row, high_row):
        copies = []
        for k, (part, row) in enumerate(((low, low_row), (high, high_row))):
            sems = refs.cc_sem.at[0, k, row], refs.cc_sem.at[1, k, row]
            source = part.at[me.core, row]
            copies.append(send(source, source, *sems, me.other_core()))
        return copies

    loads.fine.wait()
    loads.w2.wait()
    for copy in spreading:
        copy.wait()
    spreading = spread(1, low.at[me.core, me.y], high.at[me.core, me.x])
    passing = pass_on(me.y, me.x)
    for copy in halo:
        copy.wait_recv()
    for step in range(fine_tiles):
        base = step * TILE
        edges = fine[base : base + TILE, :]
        lanes = lax.broadcasted_iota(jnp.int32, (TILE, ext_rows), 1)
        picks = marks(lanes == cols[base : base + TILE, 0:1])
        sender = dot(picks, ext[...]).astype(BF16)
        refs.v_new_fine[base : base + TILE, :] = forward(
            base, edges, sender, sender_free(base, edges), None
        )
    loads.longs.wait()
    edges = longs[...]
    rest = sender_free(long_tile, edges)
    for k, by in enumerate(far_first(side)[::-1]):
        for copy in spreading[2 * (side - 2 - k) : 2 * (side - 1 - k)]:
            copy.wait()
        passing += pass_on(lax.rem(me.y + side - by, side), lax.rem(me.x + side - by, side))

    spot = cols[long_tile : long_tile + long_count, 0:1]
    spots = jnp.concatenate([spot, spot + 8], axis=0)
    core_rows = math.prod(low.shape[1:-1])
    lanes = lax.broadcasted_iota(jnp.int32, (2 * long_count, core_rows), 1)

    def coarse_rows_of(core):
        halves = jnp.zeros((2 * long_count, columns), F32)
        for k, part in enumerate((low, high)):
            here = spots - (2 * k + core) * core_rows
            halves += dot(marks(lanes == here), part[core].reshape(core_rows, columns))
        return halves

    halves = coarse_rows_of(me.core)
    for copy in passing:
        copy.wait()
    halves += coarse_rows_of(1 - me.core)
    sender = jnp.concatenate([halves[:long_count, :], halves[long_count:, :]], axis=1).astype(BF16)
    live = cols[long_tile : long_tile + long_count, 2:3].astype(F32)
    refs.v_new_long[...] = forward(long_tile, edges, sender, rest, live)

    stores = []

    def store(source, target):
        copy = pltpu.make_async_copy(source, target, refs.store_sem.at[len(stores)])
        copy.start()
        stores.append(copy)


    loads.nw1.wait()
    loads.nw2.wait()
    loads.up_nodes.wait()
    node_rows = nodes[...]
    aggregate = agg[...].astype(BF16)
    node_first = dot(node_rows, nw1[0:width, :]) + dot(aggregate, nw1[width : 2 * width, :])
    node_active, node_slope = silu_and_slope(node_first)
    node_active = node_active.astype(BF16)
    node_normed, node_inverse = norm_rows(dot(node_active, nw2[...]))
    refs.out_node[...] = (node_rows.astype(F32) + node_normed).astype(BF16)
    upstream = refs.v_up_nodes[...].astype(F32)
    ngs = norm_back(node_normed, node_inverse, upstream).astype(BF16)
    ngf = (dot_nt(ngs, nw2[...]) * node_slope).astype(BF16)
    by_node = Sum(me, refs, "n")
    per = [ref.shape[0] // patches for ref in (w1, w2, nw1, nw2)]
    by_node.put_all(per[2], dot_tn(node_active, ngs), patches)
    by_node.put_all(0, dot_tn(node_rows, ngf), patches // 2)
    by_node.put_all(0, dot_tn(aggregate, ngf), patches // 2, patches // 2)
    by_node.start()
    local = refs.local
    high_part, low_part = split(dot_nt(ngf, nw1[width : 2 * width, :]))
    ga[0:count, :] = high_part
    ga[count : 2 * count, :] = low_part

    egs_all, egf_all = refs.egs, refs.egf

    def backward(base, upstream_rows, live):
        pulled = dot(recv_cols(base), ga[...])
        if live is not None:
            pulled = pulled * live
        egn = upstream_rows.astype(F32) + pulled
        egs = norm_back(normed[base : base + TILE, :], inverse[base : base + TILE, 0:1], egn)
        normed[base : base + TILE, :] = egn
        if live is not None:
            egs = egs * live
        egs = egs.astype(BF16)
        egf = (dot_nt(egs, w2[...]) * slope[base : base + TILE, :]).astype(BF16)
        egs_all[base : base + TILE, :] = egs
        egf_all[base : base + TILE, :] = egf
        return egf

    def edge_grad(base):
        egf = egf_all[base : base + TILE, :]
        return (normed[base : base + TILE, :] + dot_nt(egf, w1[0:width, :])).astype(BF16)

    loads.up_long.wait()
    egf = backward(long_tile, up_long[...], live)
    by_coarse = Sum(me, refs, "c")
    coarse_rows = COARSE_DEV * depth
    sources = idx[3:4, long_tile : long_tile + long_count]
    for patch in range(0, patches, 4):
        spots = lax.broadcasted_iota(jnp.int32, (4 * coarse_rows, long_count), 0)
        sums = dot(marks(spots + patch * coarse_rows == sources), egf)
        by_coarse.put_all(0, sums, 4, patch)
    by_coarse.start()
    by_node.first()

    loads.up_fine.wait()
    for step in range(fine_tiles):
        base = step * TILE
        backward(base, up_fine[base : base + TILE, :], None)
    by_coarse.first()

    by_edge = Sum(me, refs, "e")
    by_edge.put_all(per[0], dot_tn(active[...], egs_all[...]), patches)
    fine_egf, long_egf = egf_all[0:fine_count, :], egf_all[fine_count:, :]
    spots = lax.broadcasted_iota(jnp.int32, (count, fine_count + long_count), 0)
    high_part, low_part = split(dot(marks(spots == idx[1:2, :]), egf_all[...]))
    grad_w1 = [
        dot_tn(fine[...], fine_egf) + dot_tn(longs[...], long_egf),
        dot_tn(senders[...], egf_all[...]),
        dot_tn(node_rows, high_part) + dot_tn(node_rows, low_part),
    ]
    grad_w1 = jnp.concatenate([part.astype(BF16) for part in grad_w1], axis=0)
    by_edge.put_all(0, grad_w1, patches)
    by_edge.start(in_pieces=True)

    spots = lax.broadcasted_iota(jnp.int32, (ext_rows, fine_count), 0)
    g_ext[...] = dot(marks(spots == idx[0:1, 0:fine_count]), fine_egf)
    halo_out, back = refs.halo_out, refs.back
    halo_out[...] = g_ext[count:ext_rows, :].astype(BF16).reshape(depth + 2, hb, width)
    returns = []
    for by in far_first(depth):
        peer = me.along_z(by)
        sems = refs.rsub_sem.at[0, by - 1], refs.rsub_sem.at[1, by - 1]
        returns.append(send(halo_out.at[peer[1]], back.at[me.z], *sems, peer))
    for k, peer in enumerate((me.previous_patch(), me.next_patch())):
        sems = refs.rpat_sem.at[0, k], refs.rpat_sem.at[1, k]
        returns.append(send(halo_out.at[depth + k], back.at[depth + k], *sems, peer))
    back[me.z] = halo_out[me.z]

    by_node.second()
    receiver_w = w1[2 * width : 3 * width, :]
    local[...] = (
        upstream
        + dot_nt(ngf, nw1[0:width, :])
        + dot_nt(high_part, receiver_w)
        + dot_nt(low_part, receiver_w)
    )
    by_edge.first()
    store(refs.v_new_fine, refs.out_fine)
    store(refs.v_new_long, refs.out_long)
    for step in range(fine_tiles - 1):
        base = step * TILE
        refs.v_gf[base : base + TILE, :] = edge_grad(base)
    by_node.across(row_blocks(by_node.patch_total()))
    by_coarse.second()
    base = fine_count - TILE
    refs.v_gf[base : base + TILE, :] = edge_grad(base)
    refs.v_gl[...] = edge_grad(long_tile)
    store(refs.v_gf, refs.out_gf)
    store(refs.v_gl, refs.out_gl)
    by_edge.second()
    by_node.share(by_node.cross_total())
    sums = by_coarse.patch_total()
    by_coarse.across(
        [
            jnp.concatenate([part[8 * k : 8 * (k + 1), :] for part in sums], axis=0)
            for k in range(depth)
        ]
    )
    for copy in returns:
        copy.wait()
    picks = marks(lax.broadcasted_iota(jnp.int32, (count, lists.shape[1]), 0) == lists[...])
    sent = g_ext[0:count, :] + dot(picks, back[...].reshape((depth + 2) * hb, width))
    by_edge.across(row_blocks(by_edge.patch_total()))

    total = by_coarse.cross_total()[0]
    coarse = jnp.concatenate([total[0:8, :], total[8:16, :]], axis=1)
    sent = jnp.concatenate([sent[0:8, :] + coarse, sent[8:, :]], axis=0)
    high_part, low_part = split(sent)
    sender_w = w1[width : 2 * width, :]
    sent_grad = dot_nt(high_part, sender_w) + dot_nt(low_part, sender_w)
    refs.out_gn[...] = (local[...] + sent_grad).astype(BF16)

    by_edge.share(by_edge.cross_total())
    for group, outs in ((by_node, (refs.out_nw1, refs.out_nw2)), (by_edge, (refs.out_w1, refs.out_w2))):
        for copy in group.sharing:
            copy.wait_recv()
        at = 0
        for out in outs:
            for row in range(0, out.shape[0], 16):
                for part in (0, 1):
                    out[row : row + 16, part * columns : (part + 1) * columns] = group.block(at)
                    at += 1
    for group in (by_node, by_coarse, by_edge):
        group.wait_sends()
    for copy in halo:
        copy.wait_send()
    for copy in stores:
        copy.wait()


def whole(side, depth, arrays):
    shapes = SimpleNamespace(**{name: array.shape for name, array in arrays.items()})
    loaded = tuple(arrays)
    count, width = shapes.nodes
    half, columns = depth // 2, width // 2
    hb = shapes.sub_list[1]
    patches = 2 * side * side
    edges = shapes.fine[0] + shapes.longs[0]
    ext_rows = count + (depth + 2) * hb
    per = [dims[0] // patches for dims in (shapes.w1, shapes.w2, shapes.nw1, shapes.nw2)]
    sem = pltpu.SemaphoreType.DMA
    vmem = pl.BlockSpec(memory_space=pltpu.VMEM)
    any_space = pl.BlockSpec(memory_space=pl.ANY)

    outs = dict(
        out_node=(shapes.nodes, BF16),
        out_fine=(shapes.fine, BF16),
        out_long=(shapes.longs, BF16),
        out_gn=(shapes.nodes, BF16),
        out_gf=(shapes.fine, BF16),
        out_gl=(shapes.longs, BF16),
        out_w1=((per[0], width), F32),
        out_w2=((per[1], width), F32),
        out_nw1=((per[2], width), F32),
        out_nw2=((per[3], width), F32),
    )
    scratch = {"v_" + n: pltpu.VMEM(arrays[n].shape, arrays[n].dtype) for n in loaded}
    scratch |= dict(
        v_new_fine=pltpu.VMEM(shapes.fine, BF16),
        v_new_long=pltpu.VMEM(shapes.longs, BF16),
        v_gf=pltpu.VMEM(shapes.fine, BF16),
        v_gl=pltpu.VMEM(shapes.longs, BF16),
        load_sem=sem((len(loaded),)),
        store_sem=sem((4,)),
        ext=pltpu.VMEM((ext_rows, width), BF16),
        low=pltpu.VMEM((2, side, side, half, 16, columns), BF16),
        high=pltpu.VMEM((2, side, side, half, 16, columns), BF16),
        rows=pltpu.VMEM((depth + 2, hb, width), BF16),
        lists=pltpu.VMEM((1, (depth + 2) * hb), jnp.int32),
        idx=pltpu.VMEM((8, edges), jnp.int32),
        cols=pltpu.VMEM((edges, 8), jnp.int32),
        slope=pltpu.VMEM((edges, width), F32),
        active=pltpu.VMEM((edges, width), BF16),
        normed=pltpu.VMEM((edges, width), F32),
        inverse=pltpu.VMEM((edges, 128), F32),
        senders=pltpu.VMEM((edges, width), BF16),
        recv_proj=pltpu.VMEM((2 * count, width), BF16),
        agg=pltpu.VMEM((count, width), F32),
        ga=pltpu.VMEM((2 * count, width), BF16),
        egs=pltpu.VMEM((edges, width), BF16),
        egf=pltpu.VMEM((edges, width), BF16),
        g_ext=pltpu.VMEM((ext_rows, width), F32),
        local=pltpu.VMEM((count, width), F32),
        halo_out=pltpu.VMEM((depth + 2, hb, width), BF16),
        back=pltpu.VMEM((depth + 2, hb, width), BF16),
        zs_sem=sem((2, depth - 1)),
        sub_sem=sem((2, depth - 1)),
        pat_sem=sem((2, 2)),
        ab_sem=sem((2, 2, 2, side - 1)),
        cc_sem=sem((2, 2, side)),
        rsub_sem=sem((2, depth - 1)),
        rpat_sem=sem((2, 2)),
    )
    groups = dict(
        n=(per[2] + per[3], 2 * (per[2] + per[3]) // 16),
        c=(COARSE_DEV * depth, depth),
        e=(per[0] + per[1], 2 * (per[0] + per[1]) // 16),
    )
    for key, (rows, blocks) in groups.items():
        for field, kind in sum_scratch(side, depth, rows, columns, blocks).items():
            scratch[key + "_" + field] = kind
    names = (*arrays, *outs, *scratch)
    return pl.pallas_call(
        functools.partial(whole_kernel, side, depth, names, loaded),
        out_shape=tuple(jax.ShapeDtypeStruct(dims, kind) for dims, kind in outs.values()),
        in_specs=[any_space] * len(arrays),
        out_specs=tuple(
            any_space if kind == BF16 and dims[0] > count else vmem for dims, kind in outs.values()
        ),
        scratch_shapes=list(scratch.values()),
        compiler_params=pltpu.CompilerParams(
            collective_id=0, has_side_effects=True, vmem_limit_bytes=VMEM_BYTES
        ),
        name="whole_layer",
    )(*arrays.values())


def hand_over_kernel(number, *refs):
    sems = refs[3 * number]
    pieces = []
    for k in range(number):
        source, target, held = refs[k], refs[number + k], refs[2 * number + k]
        for row in range(0, source.shape[0], TILE):
            rows = pl.ds(row, min(TILE, source.shape[0] - row))
            pieces.append((source.at[rows, :], held.at[rows, :], target.at[rows, :]))
    arriving, leaving = [], []
    for k, (source, held, target) in enumerate(pieces):
        arriving.append(pltpu.make_async_copy(source, held, sems.at[0, k]))
        leaving.append(pltpu.make_async_copy(held, target, sems.at[1, k]))
        arriving[k].start()
    for k in range(len(pieces)):
        arriving[k].wait()
        leaving[k].start()
    for copy in leaving:
        copy.wait()


def hand_over(results):
    number = len(results)
    any_space = pl.BlockSpec(memory_space=pl.ANY)
    return pl.pallas_call(
        functools.partial(hand_over_kernel, number),
        out_shape=tuple(jax.ShapeDtypeStruct(r.shape, r.dtype) for r in results),
        in_specs=[any_space] * number,
        out_specs=(any_space,) * number,
        scratch_shapes=[pltpu.VMEM(r.shape, r.dtype) for r in results]
        + [pltpu.SemaphoreType.DMA((2, sum(-(-r.shape[0] // TILE) for r in results)))],
        compiler_params=pltpu.CompilerParams(vmem_limit_bytes=VMEM_BYTES),
        name="hand_over",
    )(*results)


def per_device(
    side,
    depth,
    nodes,
    fine_edges,
    long_edges,
    fine_send,
    fine_recv,
    long_send,
    long_recv,
    long_mask,
    sub_list,
    patch_list,
    edge_w1,
    edge_w2,
    node_w1,
    node_w2,
    upstream_nodes,
    upstream_fine,
    upstream_long,
):
    def tiles(values):
        return values.reshape(-1, 128)

    arrays = dict(
        nodes=nodes,
        fine_send=tiles(fine_send),
        fine_recv=tiles(fine_recv),
        long_send=tiles(long_send),
        long_recv=tiles(long_recv),
        long_mask=tiles(long_mask),
        sub_list=sub_list,
        patch_list=patch_list,
        w1=edge_w1,
        fine=fine_edges,
        w2=edge_w2,
        longs=long_edges,
        nw1=node_w1,
        nw2=node_w2,
        up_nodes=upstream_nodes,
        up_long=upstream_long,
        up_fine=upstream_fine,
    )
    return hand_over(whole(side, depth, arrays))


def solution(mesh):
    side = math.isqrt(mesh.shape["patch"] // 2)
    depth = mesh.shape["sub"]
    rows = P(("patch", "sub"), None)
    flat = P(("patch", "sub"))
    return jax.shard_map(
        functools.partial(per_device, side, depth),
        mesh=mesh,
        in_specs=(rows,) * 3 + (flat,) * 5 + (rows,) * 2 + (P(),) * 4 + (rows,) * 3,
        out_specs=(rows,) * 6 + (P("patch", None),) * 4,
        check_vma=False,
    )
```
